32 devices in a mesh: group: 2 (over x), dp: 8 (over z, y), fsdp: 2 (over core).
Axes of the slice: x: 2, y: 2, z: 4, core: 2. Of those that a mesh axis runs over, the one named last changes fastest.
Arguments:
- image_tokens: bfloat16 [256, 64, 1536], P(('group', 'dp', 'fsdp')), parts along dimension 0, may hold values from -6 to 6
- text_features: bfloat16 [256, 1536], P(('group', 'dp', 'fsdp')), parts along dimension 0, may hold values from -6 to 6
- kv_weight: bfloat16 [2, 1536, 1536], P(None, None, 'fsdp'), may hold values from -0.15625 to 0.15625
- head_weight: bfloat16 [2, 1536, 1536], P(None, 'fsdp'), may hold values from -0.15625 to 0.15625
- probe: float32 [1536], replicated, may hold values from -5 to 5
- scale_key: float32 [1536], replicated, may hold values from 0.25 to 1.75
- scale_value: float32 [1536], replicated, may hold values from 0.25 to 1.75
- scale_text: float32 [1536], replicated, may hold values from 0.25 to 1.75
Outputs:
- image_grad: bfloat16 [256, 1536], P(('group', 'dp', 'fsdp')), parts along dimension 0
- text_grad: bfloat16 [256, 1536], P(('group', 'dp', 'fsdp')), parts along dimension 0
- ia3_grad: float32 [6, 1536], P('group'), parts along dimension 0
The draws below stay inside these ranges and needn't reach their ends.
There are 2 independent parts, one for each index of `group`. The reference program is written for one: setup_inputs(seed, part) draws one part's arguments, and reference() takes and returns one part's arrays. A program takes and returns all parts, laid end to end along the dimension named above; an argument that names none is the same for every part. Nothing has to cross between parts.
All inputs are finite; a program needn't handle non-finite values.
Results may differ from the reference program's by a relative error of at most 0.0058.
Values may be sent and summed in bfloat16 or wider, within the bound.
A program may use at most 128 MiB of HBM per device.

```python
import math
import jax
import jax.numpy as jnp
from jax import lax

D = 1536
HEADS = 16
HEAD_SIZE = 96
PATCHES = 64
ROWS = 8
BATCH = 128


def block_scale(key, dims, cuts, least, high):
    level = 1.0
    for position, shards_of in cuts:
        heights = jax.random.uniform(jax.random.fold_in(jax.random.fold_in(key, 6), position), (shards_of,), jnp.float32, least / len(cuts), high / len(cuts))
        level = level * jnp.repeat(jnp.exp(heights), dims[position] // shards_of).reshape((-1,) + (1,) * (len(dims) - 1 - position))
    return level


def gaussian(rng, extent, deviation, reach, split=(), held_as=jnp.bfloat16):
    values = deviation * jax.random.normal(rng, extent, jnp.float32)
    if split:
        values = values * block_scale(rng, extent, split, -0.22, 0.18)
    return jnp.clip(values, -reach, reach).astype(held_as)


def setup_inputs(seed: int = 0, part: int = 0) -> dict:
    arg_keys = jax.random.split(jax.random.key(seed), 9)
    part_keys = jax.random.split(jax.random.fold_in(arg_keys[8], part), 9)
    return {
        "image_tokens": gaussian(part_keys[0], (BATCH, PATCHES, D), 1.0, 6.0, ((0, 16),)),
        "text_features": gaussian(part_keys[1], (BATCH, D), 1.0, 6.0, ((0, 16),)),
        "kv_weight": gaussian(arg_keys[2], (2, D, D), D ** -0.5, 0.15625, ((2, 2),)),
        "head_weight": gaussian(arg_keys[3], (2, D, D), D ** -0.5, 0.15625, ((1, 2),)),
        "probe": gaussian(arg_keys[4], (D,), 1.0, 5.0, (), jnp.float32),
        "scale_key": jnp.clip(1.0 + 0.15 * jax.random.normal(arg_keys[5], (D,), jnp.float32), 0.25, 1.75),
        "scale_value": jnp.clip(1.0 + 0.15 * jax.random.normal(arg_keys[6], (D,), jnp.float32), 0.25, 1.75),
        "scale_text": jnp.clip(1.0 + 0.15 * jax.random.normal(arg_keys[7], (D,), jnp.float32), 0.25, 1.75),
    }


LOGIT_SCALE = 10.0
LOGIT_BIAS = -2.0
EPSILON = 1e-06
HIGHEST = lax.Precision.HIGHEST

def unit_norm(embedding):
    inverse = lax.rsqrt(lax.optimization_barrier(jnp.sum(embedding * embedding, axis=-1, keepdims=True)) + EPSILON)
    return (embedding * inverse, inverse)

def unit_back(unit_vec, inverse, upstream):
    return inverse * (upstream - unit_vec * lax.optimization_barrier(jnp.sum(unit_vec * upstream, axis=-1, keepdims=True)))

def pool_forward(tokens_blk, kv_weight, probe, scale_key):
    count_img = tokens_blk.shape[0]
    flat_tokens = tokens_blk.reshape(count_img * PATCHES, D)
    key_raw = jnp.dot(flat_tokens, kv_weight[0], preferred_element_type=jnp.float32)
    value_raw = jnp.dot(flat_tokens, kv_weight[1], preferred_element_type=jnp.float32)
    keys_four = (key_raw * scale_key).reshape(count_img, PATCHES, HEADS, HEAD_SIZE)
    values_four = value_raw.reshape(count_img, PATCHES, HEADS, HEAD_SIZE)
    probe_heads = probe.reshape(HEADS, HEAD_SIZE)
    scores = jnp.einsum('nphe,he->nhp', keys_four, probe_heads, precision=HIGHEST) / math.sqrt(HEAD_SIZE)
    attention = jax.nn.softmax(scores, axis=-1)
    pooled_raw = jnp.einsum('nhp,nphe->nhe', attention, values_four, precision=HIGHEST).reshape(count_img, D)
    return (attention, pooled_raw)

def key_back(tokens_blk, attention, d_pooled, kv_weight, scale_value):
    count_img = tokens_blk.shape[0]
    tokens_wide = tokens_blk.astype(jnp.float32)
    value_w = kv_weight[1].astype(jnp.float32).reshape(D, HEADS, HEAD_SIZE)
    key_w = kv_weight[0].astype(jnp.float32).reshape(D, HEADS, HEAD_SIZE)
    scaled = (d_pooled * scale_value).reshape(count_img, HEADS, HEAD_SIZE)
    direction = jnp.einsum('dhe,nhe->nhd', value_w, scaled, precision=HIGHEST)
    d_attention = jnp.einsum('npd,nhd->nhp', tokens_wide, direction, precision=HIGHEST)
    d_scores = attention * (d_attention - lax.optimization_barrier(jnp.sum(attention * d_attention, axis=-1, keepdims=True)))
    mixed_keys = jnp.einsum('nhp,npd->nhd', d_scores, tokens_wide, precision=HIGHEST)
    return jnp.einsum('nhd,dhe->he', mixed_keys, key_w, precision=HIGHEST)

def reference(image_tokens, text_features, kv_weight, head_weight, probe, scale_key, scale_value, scale_text):
    blocks = image_tokens.reshape(BATCH // ROWS, ROWS, PATCHES, D)
    attention, pooled_raw = lax.map(lambda tokens_blk: pool_forward(tokens_blk, kv_weight, probe, scale_key), blocks)
    pooled_raw = pooled_raw.reshape(BATCH, D)
    pooled = (pooled_raw * scale_value).astype(jnp.bfloat16)
    image_emb = jnp.dot(pooled, head_weight[0], preferred_element_type=jnp.float32)
    image_unit, image_inv = unit_norm(image_emb)
    text_raw = jnp.dot(text_features, head_weight[1], preferred_element_type=jnp.float32)
    text_unit, text_inv = unit_norm(text_raw * scale_text)
    image_sent = image_unit.astype(jnp.bfloat16)
    text_sent = text_unit.astype(jnp.bfloat16)
    logits = LOGIT_SCALE * jnp.dot(image_sent, text_sent.T, preferred_element_type=jnp.float32) + LOGIT_BIAS
    coeffs = (jax.nn.sigmoid(logits) - jnp.eye(BATCH, dtype=jnp.float32)).astype(jnp.bfloat16)
    image_grad = LOGIT_SCALE * jnp.dot(coeffs, text_sent, preferred_element_type=jnp.float32)
    text_grad = LOGIT_SCALE * jnp.dot(coeffs.T, image_sent, preferred_element_type=jnp.float32)
    image_back = unit_back(image_unit, image_inv, image_grad).astype(jnp.bfloat16)
    d_pooled = jnp.dot(image_back, head_weight[0].T, preferred_element_type=jnp.float32)
    grad_value = lax.optimization_barrier(jnp.sum(d_pooled * pooled_raw, axis=0))
    d_blocks = d_pooled.reshape(BATCH // ROWS, ROWS, D)
    key_parts = lax.map(lambda packed: key_back(packed[0], packed[1], packed[2], kv_weight, scale_value), (blocks, attention, d_blocks))
    grad_key = probe * lax.optimization_barrier(jnp.sum(key_parts, axis=0)).reshape(D) / math.sqrt(HEAD_SIZE)
    text_back = unit_back(text_unit, text_inv, text_grad)
    grad_text = lax.optimization_barrier(jnp.sum(text_back * text_raw, axis=0))
    ia3_grad = jnp.stack([grad_key, grad_value, grad_text]) / BATCH
    return (image_grad.astype(jnp.bfloat16), text_grad.astype(jnp.bfloat16), ia3_grad)
```

```python
import functools
import math

import jax
import jax.numpy as jnp
from jax import lax
from jax.experimental import pallas as pl
from jax.experimental.pallas import tpu as pltpu
from jax.sharding import PartitionSpec as P

HEAD_SIZE = 96
PATCHES = 64
LOGIT_SCALE = 10.0
LOGIT_BIAS = -2.0
EPSILON = 1e-06
MESH = pl.DeviceIdType.MESH
BF16 = jnp.bfloat16
F32 = jnp.float32


def mm(a, b):
    return jnp.dot(a, b, preferred_element_type=F32)


def mm_nt(a, b):
    return lax.dot_general(a, b, (((1,), (1,)), ((), ())), preferred_element_type=F32)


def split(x):
    high = x.astype(BF16)
    low = (x - high.astype(F32)).astype(BF16)
    return jnp.concatenate([high, low], axis=0)


def join(x):
    m = x.shape[0] // 2
    return x[:m] + x[m:]


def per_image(x, op, fill):
    lanes = lax.broadcasted_iota(jnp.int32, (x.shape[0], 128), 1)
    low = lanes < PATCHES
    blocks = []
    for j in range(x.shape[1] // 128):
        b = x[:, 128 * j : 128 * j + 128]
        first = op(jnp.where(low, b, fill), axis=1, keepdims=True)
        second = op(jnp.where(low, fill, b), axis=1, keepdims=True)
        blocks.append(jnp.where(low, first, second))
    return jnp.concatenate(blocks, axis=1)


def sigmoid(x):
    return 1.0 / (1.0 + jnp.exp(-x))


def kernel(
    n_dp, rows, tok_hbm, txt_hbm, kv_hbm, hw_hbm, probe_hbm, sk_hbm, sv_hbm, st_hbm,
    ig_out, tg_out, ia_out,
    tok, kw, vw, hw0, hw1, txt_in, txt, probe, sk, sv, st, tpart, ipart, all_text, all_image,
    att, ctx, fin, local_sem, tok_send, tok_recv, pair_send, pair_recv,
    text_send, text_recv, image_send, image_recv, fin_send, fin_recv,
):
    dp = lax.axis_index("dp")
    f = lax.axis_index("fsdp")
    other = 1 - f
    me = dp * 2 + f
    d_model = tok.shape[2]
    half_d = kw.shape[1]
    heads = half_d // HEAD_SIZE
    pair = 2 * rows
    half_tok = rows * PATCHES
    chunk = half_tok // 2
    n_dev = 2 * n_dp
    count = n_dp * pair

    copies = []

    def load(src, dst):
        c = pltpu.make_async_copy(src, dst, local_sem.at[len(copies)])
        c.start()
        copies.append(c)
        return c

    c_txt = load(txt_hbm, txt_in)
    c_vec = [load(probe_hbm, probe), load(sk_hbm, sk), load(sv_hbm, sv), load(st_hbm, st)]
    c_kw = load(kv_hbm.at[0], kw)
    c_tok = [
        load(tok_hbm.at[pl.ds(chunk * i, chunk)], tok.at[0, pl.ds(chunk * i, chunk)]) for i in range(2)
    ]
    c_hw1 = load(hw_hbm.at[1], hw1)
    c_vw = load(kv_hbm.at[1], vw)
    c_hw0 = load(hw_hbm.at[0], hw0)

    barrier = pltpu.get_barrier_semaphore()

    def greet(k, carry):
        peer = lax.rem(me + k, n_dev)
        pl.semaphore_signal(
            barrier, inc=1, device_id={"dp": peer // 2, "fsdp": lax.rem(peer, 2)}, device_id_type=MESH
        )
        return carry

    lax.fori_loop(1, n_dev, greet, 0)

    c_txt.wait()
    mine = pl.ds(pl.multiple_of(f * rows, rows), rows)
    txt[mine, :] = txt_in[...].astype(F32)

    pl.semaphore_wait(barrier, n_dev - 1)

    def to_partner(src, dst, send, recv):
        return pltpu.make_async_remote_copy(
            src_ref=src, dst_ref=dst, send_sem=send, recv_sem=recv,
            device_id={"fsdp": other}, device_id_type=MESH,
        )

    r_txt = to_partner(txt.at[mine], txt.at[mine], pair_send.at[0], pair_recv.at[0])
    r_txt.start()
    r_tok = []
    for i in range(2):
        r = to_partner(
            tok_hbm.at[pl.ds(chunk * i, chunk)], tok.at[1, pl.ds(chunk * i, chunk)],
            tok_send.at[i], tok_recv.at[i],
        )
        r.start()
        r_tok.append(r)

    def my_half(v):
        return jnp.where(f == 0, v[:, :half_d], v[:, half_d:])

    row_id = lax.broadcasted_iota(jnp.int32, (heads, half_d), 0)
    col_id = lax.broadcasted_iota(jnp.int32, (heads, half_d), 1)
    head_mask = ((col_id >= row_id * HEAD_SIZE) & (col_id < (row_id + 1) * HEAD_SIZE)).astype(F32)

    for c in c_vec:
        c.wait()
    probe_h = my_half(probe[...]) * (1.0 / math.sqrt(HEAD_SIZE))
    sv_h = my_half(sv[...])
    query = head_mask * (probe_h * my_half(sk[...]))
    c_kw.wait()
    query_tok = split(join(mm_nt(split(query), kw[...])))

    group = chunk // PATCHES
    ga = lax.broadcasted_iota(jnp.int32, (group, heads, chunk), 0) * PATCHES
    gb = lax.broadcasted_iota(jnp.int32, (group, heads, chunk), 2)
    block_mask = ((gb >= ga) & (gb < ga + PATCHES)).astype(F32)

    def attend(side, part):
        t = tok[side, part * chunk : (part + 1) * chunk, :]
        scores = join(mm_nt(query_tok, t))
        e = jnp.exp(scores - per_image(scores, jnp.max, -jnp.inf))
        a = e / per_image(e, jnp.sum, 0.0)
        att[side, :, part * chunk : (part + 1) * chunk] = a
        spread = (a[None] * block_mask).reshape(group * heads, chunk)
        mixed = split(join(mm(split(spread), t)))
        m = group * heads
        at = (side * 2 + part) * m
        ctx[0, at : at + m, :] = mixed[:m]
        ctx[1, at : at + m, :] = mixed[m:]

    for i in range(2):
        c_tok[i].wait()
        attend(0, i)

    c_hw1.wait()
    r_txt.wait()
    t_all = txt[...]
    tpart[0] = mm(my_half(t_all).astype(BF16), hw1[...])
    r_tp = to_partner(tpart.at[0], tpart.at[1], pair_send.at[1], pair_recv.at[1])
    r_tp.start()

    r_tok[0].wait()
    attend(1, 0)

    def unit(e):
        inv = lax.rsqrt(jnp.sum(e * e, axis=1, keepdims=True) + EPSILON)
        return e * inv, inv

    def back(u, inv, g):
        return inv * (g - u * jnp.sum(u * g, axis=1, keepdims=True))

    my_rows = pl.ds(pl.multiple_of(dp * pair, pair), pair)

    def gather_copy(buf, at, send, recv, peer):
        return pltpu.make_async_remote_copy(
            src_ref=buf.at[at], dst_ref=buf.at[at], send_sem=send, recv_sem=recv,
            device_id={"dp": peer}, device_id_type=MESH,
        )

    def gather_start(buf, send, recv):
        def body(k, carry):
            peer = lax.rem(dp + k, n_dp)
            gather_copy(buf, my_rows, send.at[peer], recv.at[dp], peer).start()
            return carry

        lax.fori_loop(1, n_dp, body, 0)

    def gather_wait(buf, send, recv):
        def body(k, carry):
            peer = lax.rem(dp + k, n_dp)
            at = pl.ds(pl.multiple_of(peer * pair, pair), pair)
            c = gather_copy(buf, at, send.at[peer], recv.at[peer], peer)
            c.wait_recv()
            c.wait_send()
            return carry

        lax.fori_loop(1, n_dp, body, 0)

    r_tp.wait()
    text_raw = tpart[0] + tpart[1]
    text_unit, text_inv = unit(text_raw * st[...])
    text_sent = text_unit.astype(BF16)
    all_text[my_rows, :] = text_sent
    gather_start(all_text, text_send, text_recv)

    r_tok[1].wait()
    attend(1, 1)

    def swap(x):
        m = x.shape[0] // 2
        return jnp.where(f == 0, x, jnp.concatenate([x[m:], x[:m]], axis=0))

    c_vw.wait()
    n_ctx = pair * heads
    pooled_all = mm(ctx[...].reshape(2 * n_ctx, d_model), vw[...])
    pooled_all = join(pooled_all).reshape(pair, heads, half_d) * head_mask[None]
    pooled_raw = swap(jnp.sum(pooled_all, axis=1))
    pooled = (pooled_raw * sv_h).astype(BF16)
    c_hw0.wait()
    ipart[0] = mm(pooled, hw0[...])
    r_ip = to_partner(ipart.at[0], ipart.at[1], pair_send.at[2], pair_recv.at[2])
    r_ip.start()

    d_row = lax.broadcasted_iota(jnp.int32, (pair, count), 0) + dp * pair
    d_col = lax.broadcasted_iota(jnp.int32, (pair, count), 1)
    diagonal = (d_row == d_col).astype(F32)

    def coefficients(sent, everyone):
        logits = LOGIT_SCALE * mm_nt(sent, everyone) + LOGIT_BIAS
        return (sigmoid(logits) - diagonal).astype(BF16)

    gather_wait(all_text, text_send, text_recv)
    r_ip.wait()
    image_unit, image_inv = unit(ipart[0] + ipart[1])
    image_sent = image_unit.astype(BF16)
    all_image[my_rows, :] = image_sent
    gather_start(all_image, image_send, image_recv)

    image_grad = LOGIT_SCALE * mm(coefficients(image_sent, all_text[...]), all_text[...])
    ig_out[...] = jnp.where(f == 0, image_grad[:rows], image_grad[rows:]).astype(BF16)
    image_back = back(image_unit, image_inv, image_grad).astype(BF16)
    d_pooled = mm_nt(image_back, hw0[...])
    grad_value = jnp.sum(d_pooled * pooled_raw, axis=0, keepdims=True)

    d_local = swap(d_pooled * sv_h)
    d_spread = (d_local[:, None, :] * head_mask[None]).reshape(n_ctx, half_d)
    direction = join(mm_nt(split(d_spread), vw[...]))
    mixed_keys = jnp.zeros((2 * heads, d_model), F32)
    m = group * heads
    for side in range(2):
        for part in range(2):
            at = (side * 2 + part) * m
            t = tok[side, part * chunk : (part + 1) * chunk, :]
            d_att = join(mm_nt(split(direction[at : at + m]), t))
            d_att = jnp.sum(d_att.reshape(group, heads, chunk) * block_mask, axis=0)
            a = att[side, :, part * chunk : (part + 1) * chunk]
            d_scores = a * (d_att - per_image(a * d_att, jnp.sum, 0.0))
            mixed_keys += mm(split(d_scores), t)
    grad_key = join(mm(split(join(mixed_keys)), kw[...]))
    grad_key = probe_h * jnp.sum(grad_key * head_mask, axis=0, keepdims=True)

    gather_wait(all_image, image_send, image_recv)
    text_grad = LOGIT_SCALE * mm(coefficients(text_sent, all_image[...]), all_image[...])
    tg_out[...] = jnp.where(f == 0, text_grad[:rows], text_grad[rows:]).astype(BF16)
    grad_text = my_half(jnp.sum(back(text_unit, text_inv, text_grad) * text_raw, axis=0, keepdims=True))

    totals = jnp.concatenate([grad_key, grad_value, grad_text], axis=0)
    tiles = half_d // 128
    fin[dp, f] = jnp.zeros(fin.shape[2:], F32)
    for j in range(tiles):
        fin[dp, f, 3 * j : 3 * j + 3, :] = totals[:, 128 * j : 128 * j + 128]

    def fin_copy(slot_dp, slot_f, send, recv, peer_dp, peer_f):
        return pltpu.make_async_remote_copy(
            src_ref=fin.at[slot_dp, slot_f], dst_ref=fin.at[slot_dp, slot_f], send_sem=send, recv_sem=recv,
            device_id={"dp": peer_dp, "fsdp": peer_f}, device_id_type=MESH,
        )

    def fin_start(k, carry):
        peer = lax.rem(me + k, n_dev)
        fin_copy(dp, f, fin_send.at[peer], fin_recv.at[me], peer // 2, lax.rem(peer, 2)).start()
        return carry

    def fin_wait(k, carry):
        peer = lax.rem(me + k, n_dev)
        peer_dp, peer_f = peer // 2, lax.rem(peer, 2)
        c = fin_copy(peer_dp, peer_f, fin_send.at[peer], fin_recv.at[peer], peer_dp, peer_f)
        c.wait_recv()
        c.wait_send()
        return carry

    lax.fori_loop(1, n_dev, fin_start, 0)
    lax.fori_loop(1, n_dev, fin_wait, 0)
    for side in range(2):
        total = jnp.sum(fin[:, side], axis=0) * (1.0 / count)
        for j in range(tiles):
            at = side * half_d + 128 * j
            ia_out[:, at : at + 128] = total[3 * j : 3 * j + 3]


def on_device(n_dp, image_tokens, text_features, kv_weight, head_weight, probe, scale_key, scale_value, scale_text):
    rows, patches, d_model = image_tokens.shape
    half_d = kv_weight.shape[2]
    heads = half_d // HEAD_SIZE
    half_tok = rows * patches
    pair = 2 * rows
    count = n_dp * pair
    dma = pltpu.SemaphoreType.DMA
    vec = (1, d_model)
    vmem = pl.BlockSpec(memory_space=pltpu.VMEM)
    return pl.pallas_call(
        functools.partial(kernel, n_dp, rows),
        out_shape=(
            jax.ShapeDtypeStruct((rows, d_model), BF16),
            jax.ShapeDtypeStruct((rows, d_model), BF16),
            jax.ShapeDtypeStruct((3, d_model), F32),
        ),
        in_specs=[pl.BlockSpec(memory_space=pl.ANY)] * 8,
        out_specs=(vmem, vmem, vmem),
        scratch_shapes=[
            pltpu.VMEM((2, half_tok, d_model), BF16),
            pltpu.VMEM((d_model, half_d), BF16),
            pltpu.VMEM((d_model, half_d), BF16),
            pltpu.VMEM((half_d, d_model), BF16),
            pltpu.VMEM((half_d, d_model), BF16),
            pltpu.VMEM((rows, d_model), BF16),
            pltpu.VMEM((pair, d_model), F32),
            pltpu.VMEM(vec, F32),
            pltpu.VMEM(vec, F32),
            pltpu.VMEM(vec, F32),
            pltpu.VMEM(vec, F32),
            pltpu.VMEM((2, pair, d_model), F32),
            pltpu.VMEM((2, pair, d_model), F32),
            pltpu.VMEM((count, d_model), BF16),
            pltpu.VMEM((count, d_model), BF16),
            pltpu.VMEM((2, heads, half_tok), F32),
            pltpu.VMEM((2, pair * heads, d_model), BF16),
            pltpu.VMEM((n_dp, 2, 24, 128), F32),
            dma((11,)),
            dma((2,)),
            dma((2,)),
            dma((3,)),
            dma((3,)),
            dma((n_dp,)),
            dma((n_dp,)),
            dma((n_dp,)),
            dma((n_dp,)),
            dma((2 * n_dp,)),
            dma((2 * n_dp,)),
        ],
        compiler_params=pltpu.CompilerParams(
            collective_id=0, has_side_effects=True, vmem_limit_bytes=56 * 1024 * 1024
        ),
    )(
        image_tokens.reshape(half_tok, d_model), text_features, kv_weight, head_weight,
        probe.reshape(vec), scale_key.reshape(vec), scale_value.reshape(vec), scale_text.reshape(vec),
    )


def solution(mesh):
    in_specs = (
        P(("group", "dp", "fsdp"), None, None),
        P(("group", "dp", "fsdp"), None),
        P(None, None, "fsdp"),
        P(None, "fsdp", None),
        P(),
        P(),
        P(),
        P(),
    )
    out_specs = (
        P(("group", "dp", "fsdp"), None),
        P(("group", "dp", "fsdp"), None),
        P("group", None),
    )
    return jax.shard_map(
        functools.partial(on_device, mesh.shape["dp"]),
        mesh=mesh, in_specs=in_specs, out_specs=out_specs, check_vma=False,
    )
```

```python
import functools
import math

import jax
import jax.numpy as jnp
from jax import lax
from jax.experimental import pallas as pl
from jax.experimental.pallas import tpu as pltpu
from jax.sharding import PartitionSpec as P

HEAD_SIZE = 96
PATCHES = 64
LOGIT_SCALE = 10.0
LOGIT_BIAS = -2.0
EPSILON = 1e-06
MESH = pl.DeviceIdType.MESH
BF16 = jnp.bfloat16
F32 = jnp.float32


def row(ref):
    return ref[...].reshape(1, ref.shape[0])


def mm(a, b):
    return jnp.dot(a, b, preferred_element_type=F32)


def mm_nt(a, b):
    return lax.dot_general(a, b, (((1,), (1,)), ((), ())), preferred_element_type=F32)


def split(x):
    high = x.astype(BF16)
    low = (x - high.astype(F32)).astype(BF16)
    return jnp.concatenate([high, low], axis=0)


def join(x):
    m = x.shape[0] // 2
    return x[:m] + x[m:]


def per_image(x, op, fill):
    lanes = lax.broadcasted_iota(jnp.int32, (x.shape[0], 128), 1)
    low = lanes < PATCHES
    blocks = []
    for j in range(x.shape[1] // 128):
        b = x[:, 128 * j : 128 * j + 128]
        first = op(jnp.where(low, b, fill), axis=1, keepdims=True)
        second = op(jnp.where(low, fill, b), axis=1, keepdims=True)
        blocks.append(jnp.where(low, first, second))
    return jnp.concatenate(blocks, axis=1)


def sigmoid(x):
    return 1.0 / (1.0 + jnp.exp(-x))


def kernel(
    n_hi, n_lo, rows, tok_hbm, txt_hbm, kv_hbm, hw_hbm, probe_hbm, sk_hbm, sv_hbm, st_hbm,
    ig_out, tg_out, ia_out,
    tok, kw, vw, hw0, hw1, txt_in, txt, probe, sk, sv, st, tpart, ipart, all_text, all_image,
    att, ctx, fin_hi, fin_lo, local_sem, tok_send, tok_recv, pair_send, pair_recv,
    text_sems, image_sems, fin_hi_send, fin_hi_recv, fin_lo_send, fin_lo_recv,
):
    dp = lax.axis_index("dp")
    f = lax.axis_index("fsdp")
    other = 1 - f
    hi, lo = dp // n_lo, lax.rem(dp, n_lo)
    n_dp = n_hi * n_lo
    square = lo * 2 + f
    d_model = tok.shape[2]
    half_d = kw.shape[1]
    heads = half_d // HEAD_SIZE
    pair = 2 * rows
    half_tok = rows * PATCHES
    chunk = half_tok // 2
    count = n_dp * pair

    copies = []

    def load(src, dst):
        c = pltpu.make_async_copy(src, dst, local_sem.at[len(copies)])
        c.start()
        copies.append(c)
        return c

    c_txt = load(txt_hbm, txt_in)
    c_hw1 = load(hw_hbm.at[1], hw1)
    c_vec = [load(probe_hbm, probe), load(sk_hbm, sk), load(sv_hbm, sv), load(st_hbm, st)]
    c_kw = load(kv_hbm.at[0], kw)
    c_tok = [
        load(tok_hbm.at[pl.ds(chunk * i, chunk)], tok.at[0, pl.ds(chunk * i, chunk)]) for i in range(2)
    ]
    c_vw = load(kv_hbm.at[1], vw)
    c_hw0 = load(hw_hbm.at[0], hw0)

    barrier = pltpu.get_barrier_semaphore()

    def at_hi(k):
        return {"dp": lax.rem(hi + k, n_hi) * n_lo + lo, "fsdp": f}

    def at_square(k):
        peer = lax.rem(square + k, 2 * n_lo)
        return {"dp": hi * n_lo + peer // 2, "fsdp": lax.rem(peer, 2)}

    def greet(where):
        def body(k, carry):
            pl.semaphore_signal(barrier, inc=1, device_id=where(k), device_id_type=MESH)
            return carry

        return body

    lax.fori_loop(1, 2 * n_lo, greet(at_square), 0)
    lax.fori_loop(1, n_hi, greet(at_hi), 0)

    c_txt.wait()
    mine = pl.ds(pl.multiple_of(f * rows, rows), rows)
    txt[mine, :] = txt_in[...].astype(F32)

    pl.semaphore_wait(barrier, 2 * n_lo - 1 + n_hi - 1)

    def to_partner(src, dst, send, recv):
        return pltpu.make_async_remote_copy(
            src_ref=src, dst_ref=dst, send_sem=send, recv_sem=recv,
            device_id={"fsdp": other}, device_id_type=MESH,
        )

    r_txt = to_partner(txt.at[mine], txt.at[mine], pair_send.at[0], pair_recv.at[0])
    r_txt.start()
    r_tok = []
    for i in range(2):
        r = to_partner(
            tok_hbm.at[pl.ds(chunk * i, chunk)], tok.at[1, pl.ds(chunk * i, chunk)],
            tok_send.at[i], tok_recv.at[i],
        )
        r.start()
        r_tok.append(r)

    def my_half(v):
        return jnp.where(f == 0, v[:, :half_d], v[:, half_d:])

    row_id = lax.broadcasted_iota(jnp.int32, (heads, half_d), 0)
    col_id = lax.broadcasted_iota(jnp.int32, (heads, half_d), 1)
    head_mask = ((col_id >= row_id * HEAD_SIZE) & (col_id < (row_id + 1) * HEAD_SIZE)).astype(F32)

    def unit(e):
        inv = lax.rsqrt(jnp.sum(e * e, axis=1, keepdims=True) + EPSILON)
        return e * inv, inv

    def back(u, inv, g):
        return inv * (g - u * jnp.sum(u * g, axis=1, keepdims=True))

    my_rows = pl.ds(pl.multiple_of(dp * pair, pair), pair)

    def gather_copy(buf, side, origin, send, recv, peer, core):
        block = buf.at[side, pl.ds(pl.multiple_of(origin * pair, pair), pair)]
        return pltpu.make_async_remote_copy(
            src_ref=block, dst_ref=block, send_sem=send, recv_sem=recv,
            device_id={"dp": peer, "fsdp": core}, device_id_type=MESH,
        )

    def each(low, high, body):
        def step(k, carry):
            body(k)
            return carry

        lax.fori_loop(low, high, step, 0)

    def gather(buf, sems):
        hi_send, lo_send, recv, core_send, core_recv = sems

        def to_hi(k):
            h = lax.rem(hi + k, n_hi)
            return gather_copy(buf, f, dp, hi_send.at[h], recv.at[dp], h * n_lo + lo, f)

        def to_lo(h, k):
            t = lax.rem(lo + k, n_lo)
            origin = h * n_lo + lo
            return gather_copy(buf, f, origin, lo_send.at[h * n_lo + t], recv.at[origin], hi * n_lo + t, f)

        def to_core(origin):
            return gather_copy(buf, f, origin, core_send.at[origin], core_recv.at[origin], dp, other)

        def arrived(origin):
            gather_copy(buf, f, origin, hi_send.at[0], recv.at[origin], dp, other).wait_recv()

        def start():
            each(1, n_hi, lambda k: to_hi(k).start())
            each(1, n_lo, lambda k: to_lo(hi, k).start())

        def forward_hi():
            def body(k):
                h = lax.rem(hi + k, n_hi)
                arrived(h * n_lo + lo)
                each(1, n_lo, lambda j: to_lo(h, j).start())
                to_core(h * n_lo + lo).start()

            each(1, n_hi, body)

        def forward_lo():
            def body(k):
                def inner(j):
                    origin = lax.rem(hi + j, n_hi) * n_lo + lax.rem(lo + k, n_lo)
                    arrived(origin)
                    to_core(origin).start()

                each(0, n_hi, inner)

            each(1, n_lo, body)

        def finish():
            def cores(k):
                origin = lax.rem(dp + k, n_dp)
                gather_copy(buf, other, origin, core_send.at[origin], core_recv.at[origin], dp, other).wait_recv()

            def sent(k):
                to_core(lax.rem(dp + k, n_dp)).wait_send()

            each(1, n_dp, cores)
            each(1, n_dp, sent)
            each(1, n_hi, lambda k: to_hi(k).wait_send())
            each(0, n_hi, lambda h: each(1, n_lo, lambda k: to_lo(h, k).wait_send()))

        return start, forward_hi, forward_lo, finish

    def place(buf, sent):
        buf[0, my_rows, :] = sent[:, :half_d]
        buf[1, my_rows, :] = sent[:, half_d:]

    def similarity(sent, buf):
        return mm_nt(sent[:, :half_d], buf[0]) + mm_nt(sent[:, half_d:], buf[1])

    def weigh(coeffs, buf):
        return LOGIT_SCALE * jnp.concatenate([mm(coeffs, buf[0]), mm(coeffs, buf[1])], axis=1)

    text_start, text_hi, text_lo, text_finish = gather(all_text, text_sems)
    image_start, image_hi, image_lo, image_finish = gather(all_image, image_sems)

    for c in c_vec:
        c.wait()
    probe_h = my_half(row(probe)) * (1.0 / math.sqrt(HEAD_SIZE))
    sv_h = my_half(row(sv))
    query = head_mask * (probe_h * my_half(row(sk)))
    c_hw1.wait()
    r_txt.wait()
    t_all = txt[...]
    tpart[0] = mm(my_half(t_all).astype(BF16), hw1[...])
    r_tp = to_partner(tpart.at[0], tpart.at[1], pair_send.at[1], pair_recv.at[1])
    r_tp.start()

    c_kw.wait()
    query_tok = split(join(mm_nt(split(query), kw[...])))

    group = chunk // PATCHES
    ga = lax.broadcasted_iota(jnp.int32, (group, heads, chunk), 0) * PATCHES
    gb = lax.broadcasted_iota(jnp.int32, (group, heads, chunk), 2)
    block_mask = ((gb >= ga) & (gb < ga + PATCHES)).astype(F32)

    def attend(side, part):
        t = tok[side, part * chunk : (part + 1) * chunk, :]
        scores = join(mm_nt(query_tok, t))
        e = jnp.exp(scores - per_image(scores, jnp.max, -jnp.inf))
        a = e / per_image(e, jnp.sum, 0.0)
        att[side, :, part * chunk : (part + 1) * chunk] = a
        spread = (a[None] * block_mask).reshape(group * heads, chunk)
        mixed = split(join(mm(split(spread), t)))
        m = group * heads
        at = (side * 2 + part) * m
        ctx[0, at : at + m, :] = mixed[:m]
        ctx[1, at : at + m, :] = mixed[m:]

    c_tok[0].wait()
    attend(0, 0)

    r_tp.wait()
    text_raw = tpart[0] + tpart[1]
    text_unit, text_inv = unit(text_raw * row(st))
    text_sent = text_unit.astype(BF16)
    place(all_text, text_sent)
    text_start()

    c_tok[1].wait()
    attend(0, 1)
    text_hi()
    r_tok[0].wait()
    attend(1, 0)
    text_lo()
    r_tok[1].wait()
    attend(1, 1)

    def swap(x):
        m = x.shape[0] // 2
        return jnp.where(f == 0, x, jnp.concatenate([x[m:], x[:m]], axis=0))

    c_vw.wait()
    n_ctx = pair * heads
    pooled_all = mm(ctx[...].reshape(2 * n_ctx, d_model), vw[...])
    pooled_all = join(pooled_all).reshape(pair, heads, half_d) * head_mask[None]
    pooled_raw = swap(jnp.sum(pooled_all, axis=1))
    pooled = (pooled_raw * sv_h).astype(BF16)
    c_hw0.wait()
    ipart[0] = mm(pooled, hw0[...])
    r_ip = to_partner(ipart.at[0], ipart.at[1], pair_send.at[2], pair_recv.at[2])
    r_ip.start()

    d_row = lax.broadcasted_iota(jnp.int32, (pair, count), 0) + dp * pair
    d_col = lax.broadcasted_iota(jnp.int32, (pair, count), 1)
    diagonal = (d_row == d_col).astype(F32)

    def coefficients(sent, buf):
        logits = LOGIT_SCALE * similarity(sent, buf) + LOGIT_BIAS
        return (sigmoid(logits) - diagonal).astype(BF16)

    text_finish()
    r_ip.wait()
    image_unit, image_inv = unit(ipart[0] + ipart[1])
    image_sent = image_unit.astype(BF16)
    place(all_image, image_sent)
    image_start()

    image_grad = weigh(coefficients(image_sent, all_text), all_text)
    ig_out[...] = jnp.where(f == 0, image_grad[:rows], image_grad[rows:]).astype(BF16)
    image_back = back(image_unit, image_inv, image_grad).astype(BF16)
    d_pooled = mm_nt(image_back, hw0[...])
    grad_value = jnp.sum(d_pooled * pooled_raw, axis=0, keepdims=True)

    image_hi()
    d_local = swap(d_pooled * sv_h)
    d_spread = (d_local[:, None, :] * head_mask[None]).reshape(n_ctx, half_d)
    direction = join(mm_nt(split(d_spread), vw[...]))
    mixed_keys = jnp.zeros((2 * heads, d_model), F32)
    m = group * heads
    for side in range(2):
        for part in range(2):
            at = (side * 2 + part) * m
            t = tok[side, part * chunk : (part + 1) * chunk, :]
            d_att = join(mm_nt(split(direction[at : at + m]), t))
            d_att = jnp.sum(d_att.reshape(group, heads, chunk) * block_mask, axis=0)
            a = att[side, :, part * chunk : (part + 1) * chunk]
            d_scores = a * (d_att - per_image(a * d_att, jnp.sum, 0.0))
            mixed_keys += mm(split(d_scores), t)
    image_lo()
    grad_key = join(mm(split(join(mixed_keys)), kw[...]))
    grad_key = probe_h * jnp.sum(grad_key * head_mask, axis=0, keepdims=True)

    image_finish()
    text_grad = weigh(coefficients(text_sent, all_image), all_image)
    tg_out[...] = jnp.where(f == 0, text_grad[:rows], text_grad[rows:]).astype(BF16)
    grad_text = my_half(jnp.sum(back(text_unit, text_inv, text_grad) * text_raw, axis=0, keepdims=True))

    totals = jnp.concatenate([grad_key, grad_value, grad_text], axis=0)
    tiles = half_d // 128
    fin_hi[hi] = jnp.zeros(fin_hi.shape[1:], F32)
    for j in range(tiles):
        fin_hi[hi, 3 * j : 3 * j + 3, :] = totals[:, 128 * j : 128 * j + 128]

    def send_hi(slot, send, recv, k):
        return pltpu.make_async_remote_copy(
            src_ref=fin_hi.at[slot], dst_ref=fin_hi.at[slot], send_sem=fin_hi_send.at[send],
            recv_sem=fin_hi_recv.at[recv], device_id=at_hi(k), device_id_type=MESH,
        )

    def send_lo(slot, send, recv, k):
        return pltpu.make_async_remote_copy(
            src_ref=fin_lo.at[slot], dst_ref=fin_lo.at[slot], send_sem=fin_lo_send.at[send],
            recv_sem=fin_lo_recv.at[recv], device_id=at_square(k), device_id_type=MESH,
        )

    def wait_hi(k):
        peer = lax.rem(hi + k, n_hi)
        c = send_hi(peer, k, peer, k)
        c.wait_recv()
        c.wait_send()

    def wait_lo(k):
        peer = lax.rem(square + k, 2 * n_lo)
        c = send_lo(peer, k, peer, k)
        c.wait_recv()
        c.wait_send()

    each(1, n_hi, lambda k: send_hi(hi, k, hi, k).start())
    each(1, n_hi, wait_hi)
    fin_lo[square] = jnp.sum(fin_hi[...], axis=0)
    each(1, 2 * n_lo, lambda k: send_lo(square, k, square, k).start())
    each(1, 2 * n_lo, wait_lo)
    for side in range(2):
        total = fin_lo[side]
        for k in range(1, n_lo):
            total = total + fin_lo[2 * k + side]
        total = total * (1.0 / count)
        for j in range(tiles):
            at = side * half_d + 128 * j
            ia_out[:, at : at + 128] = total[3 * j : 3 * j + 3]


def hand_over(ig, tg, ia, ig_out, tg_out, ia_out):
    ig_out[...] = ig[...]
    tg_out[...] = tg[...]
    ia_out[...] = ia[...]


def on_device(n_dp, image_tokens, text_features, kv_weight, head_weight, probe, scale_key, scale_value, scale_text):
    rows, patches, d_model = image_tokens.shape
    half_d = kv_weight.shape[2]
    heads = half_d // HEAD_SIZE
    half_tok = rows * patches
    pair = 2 * rows
    count = n_dp * pair
    n_lo = max(k for k in range(1, n_dp + 1) if n_dp % k == 0 and k * k <= n_dp)
    n_hi = n_dp // n_lo
    dma = pltpu.SemaphoreType.DMA
    vec = (d_model,)
    vmem = pl.BlockSpec(memory_space=pltpu.VMEM)
    out_shape = (
        jax.ShapeDtypeStruct((rows, d_model), BF16),
        jax.ShapeDtypeStruct((rows, d_model), BF16),
        jax.ShapeDtypeStruct((3, d_model), F32),
    )
    results = pl.pallas_call(
        functools.partial(kernel, n_dp // n_lo, n_lo, rows),
        out_shape=out_shape,
        in_specs=[pl.BlockSpec(memory_space=pl.ANY)] * 8,
        out_specs=(vmem, vmem, vmem),
        scratch_shapes=[
            pltpu.VMEM((2, half_tok, d_model), BF16),
            pltpu.VMEM((d_model, half_d), BF16),
            pltpu.VMEM((d_model, half_d), BF16),
            pltpu.VMEM((half_d, d_model), BF16),
            pltpu.VMEM((half_d, d_model), BF16),
            pltpu.VMEM((rows, d_model), BF16),
            pltpu.VMEM((pair, d_model), F32),
            pltpu.VMEM(vec, F32),
            pltpu.VMEM(vec, F32),
            pltpu.VMEM(vec, F32),
            pltpu.VMEM(vec, F32),
            pltpu.VMEM((2, pair, d_model), F32),
            pltpu.VMEM((2, pair, d_model), F32),
            pltpu.VMEM((2, count, half_d), BF16),
            pltpu.VMEM((2, count, half_d), BF16),
            pltpu.VMEM((2, heads, half_tok), F32),
            pltpu.VMEM((2, pair * heads, d_model), BF16),
            pltpu.VMEM((n_hi, 24, 128), F32),
            pltpu.VMEM((2 * n_lo, 24, 128), F32),
            dma((11,)),
            dma((2,)),
            dma((2,)),
            dma((3,)),
            dma((3,)),
            [dma((n_hi,)), dma((n_dp,)), dma((n_dp,)), dma((n_dp,)), dma((n_dp,))],
            [dma((n_hi,)), dma((n_dp,)), dma((n_dp,)), dma((n_dp,)), dma((n_dp,))],
            dma((n_hi,)),
            dma((n_hi,)),
            dma((2 * n_lo,)),
            dma((2 * n_lo,)),
        ],
        compiler_params=pltpu.CompilerParams(
            collective_id=0, has_side_effects=True, vmem_limit_bytes=56 * 1024 * 1024
        ),
    )(
        image_tokens.reshape(half_tok, d_model), text_features, kv_weight, head_weight,
        probe, scale_key, scale_value, scale_text,
    )
    return pl.pallas_call(
        hand_over,
        out_shape=out_shape,
        in_specs=[vmem] * 3,
        out_specs=(vmem, vmem, vmem),
        compiler_params=pltpu.CompilerParams(vmem_limit_bytes=56 * 1024 * 1024),
    )(*results)


def solution(mesh):
    in_specs = (
        P(("group", "dp", "fsdp"), None, None),
        P(("group", "dp", "fsdp"), None),
        P(None, None, "fsdp"),
        P(None, "fsdp", None),
        P(),
        P(),
        P(),
        P(),
    )
    out_specs = (
        P(("group", "dp", "fsdp"), None),
        P(("group", "dp", "fsdp"), None),
        P("group", None),
    )
    return jax.shard_map(
        functools.partial(on_device, mesh.shape["dp"]),
        mesh=mesh, in_specs=in_specs, out_specs=out_specs, check_vma=False,
    )
```

```python
import functools
import math

import jax
import jax.numpy as jnp
from jax import lax
from jax.experimental import pallas as pl
from jax.experimental.pallas import tpu as pltpu
from jax.sharding import PartitionSpec as P

HEAD_SIZE = 96
PATCHES = 64
LOGIT_SCALE = 10.0
LOGIT_BIAS = -2.0
EPSILON = 1e-06
MESH = pl.DeviceIdType.MESH
BF16 = jnp.bfloat16
F32 = jnp.float32


def row(ref):
    return ref[...].reshape(1, ref.shape[0])


def mm(a, b):
    return jnp.dot(a, b, preferred_element_type=F32)


def mm_nt(a, b):
    return lax.dot_general(a, b, (((1,), (1,)), ((), ())), preferred_element_type=F32)


def split(x):
    high = x.astype(BF16)
    low = (x - high.astype(F32)).astype(BF16)
    return jnp.concatenate([high, low], axis=0)


def join(x):
    m = x.shape[0] // 2
    return x[:m] + x[m:]


def per_image(x, op, fill):
    lanes = lax.broadcasted_iota(jnp.int32, (x.shape[0], 128), 1)
    low = lanes < PATCHES
    blocks = []
    for j in range(x.shape[1] // 128):
        b = x[:, 128 * j : 128 * j + 128]
        first = op(jnp.where(low, b, fill), axis=1, keepdims=True)
        second = op(jnp.where(low, fill, b), axis=1, keepdims=True)
        blocks.append(jnp.where(low, first, second))
    return jnp.concatenate(blocks, axis=1)


def sigmoid(x):
    return 1.0 / (1.0 + jnp.exp(-x))


def kernel(
    n_hi, n_lo, rows, tok_hbm, txt_hbm, kv_hbm, hw_hbm, probe_hbm, sk_hbm, sv_hbm, st_hbm,
    ig_out, tg_out, ia_out,
    tok, kw, vw, hw0, hw1, txt_in, txt, probe, sk, sv, st, tpart, ipart, all_text, all_image,
    att, ctx, fin_kv, fin_text, local_sem, tok_send, tok_recv, pair_send, pair_recv,
    text_sems, image_sems, kv_send, kv_recv, ft_send, ft_recv,
):
    dp = lax.axis_index("dp")
    f = lax.axis_index("fsdp")
    other = 1 - f
    hi, lo = dp // n_lo, lax.rem(dp, n_lo)
    n_dp = n_hi * n_lo
    d_model = tok.shape[2]
    half_d = kw.shape[1]
    heads = half_d // HEAD_SIZE
    pair = 2 * rows
    half_tok = rows * PATCHES
    chunk = half_tok // 2
    count = n_dp * pair

    copies = []

    def load(src, dst):
        c = pltpu.make_async_copy(src, dst, local_sem.at[len(copies)])
        c.start()
        copies.append(c)
        return c

    c_txt = load(txt_hbm, txt_in)
    c_hw1 = load(hw_hbm.at[1], hw1)
    c_vec = [load(probe_hbm, probe), load(sk_hbm, sk), load(sv_hbm, sv), load(st_hbm, st)]
    c_kw = load(kv_hbm.at[0], kw)
    c_tok = [
        load(tok_hbm.at[pl.ds(chunk * i, chunk)], tok.at[0, pl.ds(chunk * i, chunk)]) for i in range(2)
    ]
    c_vw = load(kv_hbm.at[1], vw)
    c_hw0 = load(hw_hbm.at[0], hw0)

    barrier = pltpu.get_barrier_semaphore()

    me = dp * 2 + f
    n_dev = 2 * n_dp

    def each(low, high, body):
        def step(k, carry):
            body(k)
            return carry

        lax.fori_loop(low, high, step, 0)

    def device(k):
        peer = lax.rem(me + k, n_dev)
        return {"dp": peer // 2, "fsdp": lax.rem(peer, 2)}

    each(
        1, n_dev,
        lambda k: pl.semaphore_signal(barrier, inc=1, device_id=device(k), device_id_type=MESH),
    )

    c_txt.wait()
    mine = pl.ds(pl.multiple_of(f * rows, rows), rows)
    txt[mine, :] = txt_in[...].astype(F32)

    pl.semaphore_wait(barrier, n_dev - 1)

    def to_partner(src, dst, send, recv):
        return pltpu.make_async_remote_copy(
            src_ref=src, dst_ref=dst, send_sem=send, recv_sem=recv,
            device_id={"fsdp": other}, device_id_type=MESH,
        )

    r_txt = to_partner(txt.at[mine], txt.at[mine], pair_send.at[0], pair_recv.at[0])
    r_txt.start()
    r_tok = []
    for i in range(2):
        r = to_partner(
            tok_hbm.at[pl.ds(chunk * i, chunk)], tok.at[1, pl.ds(chunk * i, chunk)],
            tok_send.at[i], tok_recv.at[i],
        )
        r.start()
        r_tok.append(r)

    def my_half(v):
        return jnp.where(f == 0, v[:, :half_d], v[:, half_d:])

    row_id = lax.broadcasted_iota(jnp.int32, (heads, half_d), 0)
    col_id = lax.broadcasted_iota(jnp.int32, (heads, half_d), 1)
    head_mask = ((col_id >= row_id * HEAD_SIZE) & (col_id < (row_id + 1) * HEAD_SIZE)).astype(F32)

    def unit(e):
        inv = lax.rsqrt(jnp.sum(e * e, axis=1, keepdims=True) + EPSILON)
        return e * inv, inv

    def back(u, inv, g):
        return inv * (g - u * jnp.sum(u * g, axis=1, keepdims=True))

    my_rows = pl.ds(pl.multiple_of(dp * pair, pair), pair)

    def gather_copy(buf, side, origin, send, recv, peer, core):
        block = buf.at[side, pl.ds(pl.multiple_of(origin * pair, pair), pair)]
        return pltpu.make_async_remote_copy(
            src_ref=block, dst_ref=block, send_sem=send, recv_sem=recv,
            device_id={"dp": peer, "fsdp": core}, device_id_type=MESH,
        )

    def gather(buf, sems):
        hi_send, lo_send, recv, core_send, core_recv = sems

        def to_hi(k):
            h = lax.rem(hi + k, n_hi)
            return gather_copy(buf, f, dp, hi_send.at[h], recv.at[dp], h * n_lo + lo, f)

        def to_lo(h, k):
            t = lax.rem(lo + k, n_lo)
            origin = h * n_lo + lo
            return gather_copy(buf, f, origin, lo_send.at[h * n_lo + t], recv.at[origin], hi * n_lo + t, f)

        def to_core(origin):
            return gather_copy(buf, f, origin, core_send.at[origin], core_recv.at[origin], dp, other)

        def arrived(origin):
            gather_copy(buf, f, origin, hi_send.at[0], recv.at[origin], dp, other).wait_recv()

        def start():
            each(1, n_hi, lambda k: to_hi(k).start())
            each(1, n_lo, lambda k: to_lo(hi, k).start())

        def forward_hi():
            def body(k):
                h = lax.rem(hi + k, n_hi)
                arrived(h * n_lo + lo)
                each(1, n_lo, lambda j: to_lo(h, j).start())
                to_core(h * n_lo + lo).start()

            each(1, n_hi, body)

        def forward_lo():
            def body(k):
                def inner(j):
                    origin = lax.rem(hi + j, n_hi) * n_lo + lax.rem(lo + k, n_lo)
                    arrived(origin)
                    to_core(origin).start()

                each(0, n_hi, inner)

            each(1, n_lo, body)

        def finish():
            def cores(k):
                origin = lax.rem(dp + k, n_dp)
                gather_copy(buf, other, origin, core_send.at[origin], core_recv.at[origin], dp, other).wait_recv()

            def sent(k):
                to_core(lax.rem(dp + k, n_dp)).wait_send()

            each(1, n_dp, cores)
            each(1, n_dp, sent)
            each(1, n_hi, lambda k: to_hi(k).wait_send())
            each(0, n_hi, lambda h: each(1, n_lo, lambda k: to_lo(h, k).wait_send()))

        return start, forward_hi, forward_lo, finish

    def place(buf, sent):
        buf[0, my_rows, :] = sent[:, :half_d]
        buf[1, my_rows, :] = sent[:, half_d:]

    def similarity(sent, buf):
        return mm_nt(sent[:, :half_d], buf[0]) + mm_nt(sent[:, half_d:], buf[1])

    def weigh(coeffs, buf):
        return LOGIT_SCALE * jnp.concatenate([mm(coeffs, buf[0]), mm(coeffs, buf[1])], axis=1)

    text_start, text_hi, text_lo, text_finish = gather(all_text, text_sems)
    image_start, image_hi, image_lo, image_finish = gather(all_image, image_sems)

    for c in c_vec:
        c.wait()
    probe_h = my_half(row(probe)) * (1.0 / math.sqrt(HEAD_SIZE))
    sv_h = my_half(row(sv))
    query = head_mask * (probe_h * my_half(row(sk)))
    c_hw1.wait()
    r_txt.wait()
    t_all = txt[...]
    tpart[0] = mm(my_half(t_all).astype(BF16), hw1[...])
    r_tp = to_partner(tpart.at[0], tpart.at[1], pair_send.at[1], pair_recv.at[1])
    r_tp.start()

    c_kw.wait()
    query_tok = split(join(mm_nt(split(query), kw[...])))

    group = chunk // PATCHES
    ga = lax.broadcasted_iota(jnp.int32, (group, heads, chunk), 0) * PATCHES
    gb = lax.broadcasted_iota(jnp.int32, (group, heads, chunk), 2)
    block_mask = ((gb >= ga) & (gb < ga + PATCHES)).astype(F32)

    def attend(side, part):
        t = tok[side, part * chunk : (part + 1) * chunk, :]
        scores = join(mm_nt(query_tok, t))
        e = jnp.exp(scores - per_image(scores, jnp.max, -jnp.inf))
        a = e / per_image(e, jnp.sum, 0.0)
        att[side, :, part * chunk : (part + 1) * chunk] = a
        spread = (a[None] * block_mask).reshape(group * heads, chunk)
        mixed = split(join(mm(split(spread), t)))
        m = group * heads
        at = (side * 2 + part) * m
        ctx[0, at : at + m, :] = mixed[:m]
        ctx[1, at : at + m, :] = mixed[m:]

    c_tok[0].wait()
    attend(0, 0)

    r_tp.wait()
    text_raw = tpart[0] + tpart[1]
    text_unit, text_inv = unit(text_raw * row(st))
    text_sent = text_unit.astype(BF16)
    place(all_text, text_sent)
    text_start()

    c_tok[1].wait()
    attend(0, 1)
    r_tok[0].wait()
    attend(1, 0)
    r_tok[1].wait()
    attend(1, 1)

    def swap(x):
        m = x.shape[0] // 2
        return jnp.where(f == 0, x, jnp.concatenate([x[m:], x[:m]], axis=0))

    c_vw.wait()
    n_ctx = pair * heads
    pooled_all = mm(ctx[...].reshape(2 * n_ctx, d_model), vw[...])
    pooled_all = join(pooled_all).reshape(pair, heads, half_d) * head_mask[None]
    pooled_raw = swap(jnp.sum(pooled_all, axis=1))
    pooled = (pooled_raw * sv_h).astype(BF16)
    c_hw0.wait()
    ipart[0] = mm(pooled, hw0[...])
    r_ip = to_partner(ipart.at[0], ipart.at[1], pair_send.at[2], pair_recv.at[2])
    r_ip.start()

    d_row = lax.broadcasted_iota(jnp.int32, (pair, count), 0) + dp * pair
    d_col = lax.broadcasted_iota(jnp.int32, (pair, count), 1)
    diagonal = (d_row == d_col).astype(F32)

    def coefficients(sent, buf):
        logits = LOGIT_SCALE * similarity(sent, buf) + LOGIT_BIAS
        return (sigmoid(logits) - diagonal).astype(BF16)

    text_hi()
    text_lo()
    r_ip.wait()
    image_unit, image_inv = unit(ipart[0] + ipart[1])
    image_sent = image_unit.astype(BF16)
    place(all_image, image_sent)
    image_start()
    text_finish()

    image_grad = weigh(coefficients(image_sent, all_text), all_text)
    ig_out[...] = jnp.where(f == 0, image_grad[:rows], image_grad[rows:]).astype(BF16)
    image_back = back(image_unit, image_inv, image_grad).astype(BF16)
    d_pooled = mm_nt(image_back, hw0[...])
    grad_value = jnp.sum(d_pooled * pooled_raw, axis=0, keepdims=True)

    d_local = swap(d_pooled * sv_h)
    d_spread = (d_local[:, None, :] * head_mask[None]).reshape(n_ctx, half_d)
    direction = join(mm_nt(split(d_spread), vw[...]))
    mixed_keys = jnp.zeros((2 * heads, d_model), F32)
    m = group * heads
    for side in range(2):
        for part in range(2):
            at = (side * 2 + part) * m
            t = tok[side, part * chunk : (part + 1) * chunk, :]
            d_att = join(mm_nt(split(direction[at : at + m]), t))
            d_att = jnp.sum(d_att.reshape(group, heads, chunk) * block_mask, axis=0)
            a = att[side, :, part * chunk : (part + 1) * chunk]
            d_scores = a * (d_att - per_image(a * d_att, jnp.sum, 0.0))
            mixed_keys += mm(split(d_scores), t)
    image_hi()
    image_lo()
    grad_key = join(mm(split(join(mixed_keys)), kw[...]))
    grad_key = probe_h * jnp.sum(grad_key * head_mask, axis=0, keepdims=True)

    tiles = half_d // 128

    def put(buf, x):
        buf[me] = jnp.zeros(buf.shape[1:], F32)
        n = x.shape[0]
        for j in range(tiles):
            buf[me, n * j : n * j + n, :] = x[:, 128 * j : 128 * j + 128]

    def total_copy(buf, slot, send, recv, k):
        return pltpu.make_async_remote_copy(
            src_ref=buf.at[slot], dst_ref=buf.at[slot], send_sem=send, recv_sem=recv,
            device_id=device(k), device_id_type=MESH,
        )

    def total_start(buf, send, recv):
        each(1, n_dev, lambda k: total_copy(buf, me, send.at[k], recv.at[me], k).start())

    def total_wait(buf, send, recv):
        def body(k):
            peer = lax.rem(me + k, n_dev)
            c = total_copy(buf, peer, send.at[k], recv.at[peer], k)
            c.wait_recv()
            c.wait_send()

        each(1, n_dev, body)

    put(fin_kv, jnp.concatenate([grad_key, grad_value], axis=0))
    total_start(fin_kv, kv_send, kv_recv)

    image_finish()
    text_grad = weigh(coefficients(text_sent, all_image), all_image)
    tg_out[...] = jnp.where(f == 0, text_grad[:rows], text_grad[rows:]).astype(BF16)
    grad_text = my_half(jnp.sum(back(text_unit, text_inv, text_grad) * text_raw, axis=0, keepdims=True))

    put(fin_text, grad_text)
    total_start(fin_text, ft_send, ft_recv)

    def write(buf, n, at):
        for side in range(2):
            total = buf[side]
            for k in range(1, n_dp):
                total = total + buf[2 * k + side]
            total = total * (1.0 / count)
            for j in range(tiles):
                start = side * half_d + 128 * j
                ia_out[at : at + n, start : start + 128] = total[n * j : n * j + n]

    total_wait(fin_kv, kv_send, kv_recv)
    write(fin_kv, 2, 0)
    total_wait(fin_text, ft_send, ft_recv)
    write(fin_text, 1, 2)


def hand_over(ig, tg, ia, ig_out, tg_out, ia_out):
    ig_out[...] = ig[...]
    tg_out[...] = tg[...]
    ia_out[...] = ia[...]


def on_device(n_dp, image_tokens, text_features, kv_weight, head_weight, probe, scale_key, scale_value, scale_text):
    rows, patches, d_model = image_tokens.shape
    half_d = kv_weight.shape[2]
    heads = half_d // HEAD_SIZE
    half_tok = rows * patches
    pair = 2 * rows
    count = n_dp * pair
    kv_rows, text_rows = (-(-n * half_d // 1024) * 8 for n in (2, 1))
    n_lo = 1
    n_hi = n_dp // n_lo
    dma = pltpu.SemaphoreType.DMA
    vec = (d_model,)
    vmem = pl.BlockSpec(memory_space=pltpu.VMEM)
    out_shape = (
        jax.ShapeDtypeStruct((rows, d_model), BF16),
        jax.ShapeDtypeStruct((rows, d_model), BF16),
        jax.ShapeDtypeStruct((3, d_model), F32),
    )
    results = pl.pallas_call(
        functools.partial(kernel, n_dp // n_lo, n_lo, rows),
        out_shape=out_shape,
        in_specs=[pl.BlockSpec(memory_space=pl.ANY)] * 8,
        out_specs=(vmem, vmem, vmem),
        scratch_shapes=[
            pltpu.VMEM((2, half_tok, d_model), BF16),
            pltpu.VMEM((d_model, half_d), BF16),
            pltpu.VMEM((d_model, half_d), BF16),
            pltpu.VMEM((half_d, d_model), BF16),
            pltpu.VMEM((half_d, d_model), BF16),
            pltpu.VMEM((rows, d_model), BF16),
            pltpu.VMEM((pair, d_model), F32),
            pltpu.VMEM(vec, F32),
            pltpu.VMEM(vec, F32),
            pltpu.VMEM(vec, F32),
            pltpu.VMEM(vec, F32),
            pltpu.VMEM((2, pair, d_model), F32),
            pltpu.VMEM((2, pair, d_model), F32),
            pltpu.VMEM((2, count, half_d), BF16),
            pltpu.VMEM((2, count, half_d), BF16),
            pltpu.VMEM((2, heads, half_tok), F32),
            pltpu.VMEM((2, pair * heads, d_model), BF16),
            pltpu.VMEM((2 * n_dp, kv_rows, 128), F32),
            pltpu.VMEM((2 * n_dp, text_rows, 128), F32),
            dma((11,)),
            dma((2,)),
            dma((2,)),
            dma((3,)),
            dma((3,)),
            [dma((n_hi,)), dma((n_dp,)), dma((n_dp,)), dma((n_dp,)), dma((n_dp,))],
            [dma((n_hi,)), dma((n_dp,)), dma((n_dp,)), dma((n_dp,)), dma((n_dp,))],
            dma((2 * n_dp,)),
            dma((2 * n_dp,)),
            dma((2 * n_dp,)),
            dma((2 * n_dp,)),
        ],
        compiler_params=pltpu.CompilerParams(
            collective_id=0, has_side_effects=True, vmem_limit_bytes=56 * 1024 * 1024
        ),
    )(
        image_tokens.reshape(half_tok, d_model), text_features, kv_weight, head_weight,
        probe, scale_key, scale_value, scale_text,
    )
    return pl.pallas_call(
        hand_over,
        out_shape=out_shape,
        in_specs=[vmem] * 3,
        out_specs=(vmem, vmem, vmem),
        compiler_params=pltpu.CompilerParams(vmem_limit_bytes=56 * 1024 * 1024),
    )(*results)


def solution(mesh):
    in_specs = (
        P(("group", "dp", "fsdp"), None, None),
        P(("group", "dp", "fsdp"), None),
        P(None, None, "fsdp"),
        P(None, "fsdp", None),
        P(),
        P(),
        P(),
        P(),
    )
    out_specs = (
        P(("group", "dp", "fsdp"), None),
        P(("group", "dp", "fsdp"), None),
        P("group", None),
    )
    return jax.shard_map(
        functools.partial(on_device, mesh.shape["dp"]),
        mesh=mesh, in_specs=in_specs, out_specs=out_specs, check_vma=False,
    )
```

```python
import functools
import math

import jax
import jax.numpy as jnp
from jax import lax
from jax.experimental import pallas as pl
from jax.experimental.pallas import tpu as pltpu
from jax.sharding import PartitionSpec as P

HEAD_SIZE = 96
PATCHES = 64
LOGIT_SCALE = 10.0
LOGIT_BIAS = -2.0
EPSILON = 1e-06
MESH = pl.DeviceIdType.MESH
BF16 = jnp.bfloat16
F32 = jnp.float32


def row(ref):
    return ref[...].reshape(1, ref.shape[0])


def mm(a, b):
    return jnp.dot(a, b, preferred_element_type=F32)


def mm_nt(a, b):
    return lax.dot_general(a, b, (((1,), (1,)), ((), ())), preferred_element_type=F32)


def split(x):
    high = x.astype(BF16)
    low = (x - high.astype(F32)).astype(BF16)
    return jnp.concatenate([high, low], axis=0)


def join(x):
    m = x.shape[0] // 2
    return x[:m] + x[m:]


def per_image(x, op, fill):
    lanes = lax.broadcasted_iota(jnp.int32, (x.shape[0], 128), 1)
    low = lanes < PATCHES
    blocks = []
    for j in range(x.shape[1] // 128):
        b = x[:, 128 * j : 128 * j + 128]
        first = op(jnp.where(low, b, fill), axis=1, keepdims=True)
        second = op(jnp.where(low, fill, b), axis=1, keepdims=True)
        blocks.append(jnp.where(low, first, second))
    return jnp.concatenate(blocks, axis=1)


def sigmoid(x):
    return 1.0 / (1.0 + jnp.exp(-x))


def kernel(
    n_hi, n_lo, rows, tok_hbm, txt_hbm, kv_hbm, hw_hbm, probe_hbm, sk_hbm, sv_hbm, st_hbm,
    ig_out, tg_out, ia_out,
    tok, kw, vw, hw0, hw1, txt_in, txt, probe, sk, sv, st, tpart, ipart, all_text, all_image,
    att, ctx, fin_kv, fin_text, local_sem, tok_send, tok_recv, pair_send, pair_recv,
    text_sems, image_sems, kv_send, kv_recv, ft_send, ft_recv,
):
    dp = lax.axis_index("dp")
    f = lax.axis_index("fsdp")
    other = 1 - f
    hi, lo = dp // n_lo, lax.rem(dp, n_lo)
    n_dp = n_hi * n_lo
    d_model = tok.shape[2]
    half_d = kw.shape[1]
    heads = half_d // HEAD_SIZE
    pair = 2 * rows
    half_tok = rows * PATCHES
    chunk = half_tok // 2
    count = n_dp * pair

    copies = []

    def load(src, dst):
        c = pltpu.make_async_copy(src, dst, local_sem.at[len(copies)])
        c.start()
        copies.append(c)
        return c

    c_txt = load(txt_hbm, txt_in)
    c_vec = [load(probe_hbm, probe), load(sk_hbm, sk), load(sv_hbm, sv), load(st_hbm, st)]
    c_kw = load(kv_hbm.at[0], kw)
    c_hw1 = load(hw_hbm.at[1], hw1)
    c_tok = [
        load(tok_hbm.at[pl.ds(chunk * i, chunk)], tok.at[0, pl.ds(chunk * i, chunk)]) for i in range(2)
    ]
    c_vw = load(kv_hbm.at[1], vw)
    c_hw0 = load(hw_hbm.at[0], hw0)

    barrier = pltpu.get_barrier_semaphore()

    me = dp * 2 + f
    n_dev = 2 * n_dp

    def each(low, high, body):
        def step(k, carry):
            body(k)
            return carry

        lax.fori_loop(low, high, step, 0)

    def device(k):
        peer = lax.rem(me + k, n_dev)
        return {"dp": peer // 2, "fsdp": lax.rem(peer, 2)}

    each(
        1, n_dev,
        lambda k: pl.semaphore_signal(barrier, inc=1, device_id=device(k), device_id_type=MESH),
    )

    c_txt.wait()
    mine = pl.ds(pl.multiple_of(f * rows, rows), rows)
    txt[mine, :] = txt_in[...].astype(F32)

    def my_half(v):
        return jnp.where(f == 0, v[:, :half_d], v[:, half_d:])

    row_id = lax.broadcasted_iota(jnp.int32, (heads, half_d), 0)
    col_id = lax.broadcasted_iota(jnp.int32, (heads, half_d), 1)
    head_mask = ((col_id >= row_id * HEAD_SIZE) & (col_id < (row_id + 1) * HEAD_SIZE)).astype(F32)

    for c in c_vec:
        c.wait()
    probe_h = my_half(row(probe)) * (1.0 / math.sqrt(HEAD_SIZE))
    sv_h = my_half(row(sv))
    query = head_mask * (probe_h * my_half(row(sk)))
    c_kw.wait()
    query_tok = split(join(mm_nt(split(query), kw[...])))

    pl.semaphore_wait(barrier, n_dev - 1)

    def to_partner(src, dst, send, recv):
        return pltpu.make_async_remote_copy(
            src_ref=src, dst_ref=dst, send_sem=send, recv_sem=recv,
            device_id={"fsdp": other}, device_id_type=MESH,
        )

    r_txt = to_partner(txt.at[mine], txt.at[mine], pair_send.at[0], pair_recv.at[0])
    r_txt.start()
    r_tok = []
    for i in range(2):
        r = to_partner(
            tok_hbm.at[pl.ds(chunk * i, chunk)], tok.at[1, pl.ds(chunk * i, chunk)],
            tok_send.at[i], tok_recv.at[i],
        )
        r.start()
        r_tok.append(r)

    def unit(e):
        inv = lax.rsqrt(jnp.sum(e * e, axis=1, keepdims=True) + EPSILON)
        return e * inv, inv

    def back(u, inv, g):
        return inv * (g - u * jnp.sum(u * g, axis=1, keepdims=True))

    my_rows = pl.ds(pl.multiple_of(dp * pair, pair), pair)

    def gather_copy(buf, side, origin, send, recv, peer, core):
        block = buf.at[side, pl.ds(pl.multiple_of(origin * pair, pair), pair)]
        return pltpu.make_async_remote_copy(
            src_ref=block, dst_ref=block, send_sem=send, recv_sem=recv,
            device_id={"dp": peer, "fsdp": core}, device_id_type=MESH,
        )

    def gather(buf, sems):
        hi_send, lo_send, recv, core_send, core_recv = sems

        def to_hi(k):
            h = lax.rem(hi + k, n_hi)
            return gather_copy(buf, f, dp, hi_send.at[h], recv.at[dp], h * n_lo + lo, f)

        def to_lo(h, k):
            t = lax.rem(lo + k, n_lo)
            origin = h * n_lo + lo
            return gather_copy(buf, f, origin, lo_send.at[h * n_lo + t], recv.at[origin], hi * n_lo + t, f)

        def to_core(origin):
            return gather_copy(buf, f, origin, core_send.at[origin], core_recv.at[origin], dp, other)

        def arrived(origin):
            gather_copy(buf, f, origin, hi_send.at[0], recv.at[origin], dp, other).wait_recv()

        def start():
            each(1, n_hi, lambda k: to_hi(k).start())
            each(1, n_lo, lambda k: to_lo(hi, k).start())

        def forward_hi():
            def body(k):
                h = lax.rem(hi + k, n_hi)
                arrived(h * n_lo + lo)
                each(1, n_lo, lambda j: to_lo(h, j).start())
                to_core(h * n_lo + lo).start()

            each(1, n_hi, body)

        def forward_lo():
            def body(k):
                def inner(j):
                    origin = lax.rem(hi + j, n_hi) * n_lo + lax.rem(lo + k, n_lo)
                    arrived(origin)
                    to_core(origin).start()

                each(0, n_hi, inner)

            each(1, n_lo, body)

        def finish():
            def cores(k):
                origin = lax.rem(dp + k, n_dp)
                gather_copy(buf, other, origin, core_send.at[origin], core_recv.at[origin], dp, other).wait_recv()

            def sent(k):
                to_core(lax.rem(dp + k, n_dp)).wait_send()

            each(1, n_dp, cores)
            each(1, n_dp, sent)
            each(1, n_hi, lambda k: to_hi(k).wait_send())
            each(0, n_hi, lambda h: each(1, n_lo, lambda k: to_lo(h, k).wait_send()))

        return start, forward_hi, forward_lo, finish

    def place(buf, sent):
        buf[0, my_rows, :] = sent[:, :half_d]
        buf[1, my_rows, :] = sent[:, half_d:]

    def similarity(sent, buf):
        return mm_nt(sent[:, :half_d], buf[0]) + mm_nt(sent[:, half_d:], buf[1])

    def weigh(coeffs, buf):
        return LOGIT_SCALE * jnp.concatenate([mm(coeffs, buf[0]), mm(coeffs, buf[1])], axis=1)

    text_start, text_hi, text_lo, text_finish = gather(all_text, text_sems)
    image_start, image_hi, image_lo, image_finish = gather(all_image, image_sems)

    c_hw1.wait()
    r_txt.wait()
    t_all = txt[...]
    tpart[0] = mm(my_half(t_all).astype(BF16), hw1[...])
    r_tp = to_partner(tpart.at[0], tpart.at[1], pair_send.at[1], pair_recv.at[1])
    r_tp.start()

    group = chunk // PATCHES
    ga = lax.broadcasted_iota(jnp.int32, (group, heads, chunk), 0) * PATCHES
    gb = lax.broadcasted_iota(jnp.int32, (group, heads, chunk), 2)
    block_mask = ((gb >= ga) & (gb < ga + PATCHES)).astype(F32)

    def attend(side):
        scores = join(mm_nt(query_tok, tok[side]))
        e = jnp.exp(scores - per_image(scores, jnp.max, -jnp.inf))
        a = e / per_image(e, jnp.sum, 0.0)
        att[side] = a
        m = group * heads
        for part in range(2):
            spread = (a[None, :, part * chunk : (part + 1) * chunk] * block_mask).reshape(m, chunk)
            mixed = split(join(mm(split(spread), tok[side, part * chunk : (part + 1) * chunk, :])))
            at = (side * 2 + part) * m
            ctx[0, at : at + m, :] = mixed[:m]
            ctx[1, at : at + m, :] = mixed[m:]

    c_tok[0].wait()
    c_tok[1].wait()
    attend(0)

    r_tp.wait()
    text_raw = tpart[0] + tpart[1]
    text_unit, text_inv = unit(text_raw * row(st))
    text_sent = text_unit.astype(BF16)
    place(all_text, text_sent)
    text_start()

    r_tok[0].wait()
    r_tok[1].wait()
    attend(1)

    def swap(x):
        m = x.shape[0] // 2
        return jnp.where(f == 0, x, jnp.concatenate([x[m:], x[:m]], axis=0))

    c_vw.wait()
    n_ctx = pair * heads
    pooled_all = mm(ctx[...].reshape(2 * n_ctx, d_model), vw[...])
    pooled_all = join(pooled_all).reshape(pair, heads, half_d) * head_mask[None]
    pooled_raw = swap(jnp.sum(pooled_all, axis=1))
    pooled = (pooled_raw * sv_h).astype(BF16)
    c_hw0.wait()
    ipart[0] = mm(pooled, hw0[...])
    r_ip = to_partner(ipart.at[0], ipart.at[1], pair_send.at[2], pair_recv.at[2])
    r_ip.start()

    d_row = lax.broadcasted_iota(jnp.int32, (pair, count), 0) + dp * pair
    d_col = lax.broadcasted_iota(jnp.int32, (pair, count), 1)
    diagonal = (d_row == d_col).astype(F32)

    def coefficients(sent, buf):
        logits = LOGIT_SCALE * similarity(sent, buf) + LOGIT_BIAS
        return (sigmoid(logits) - diagonal).astype(BF16)

    text_hi()
    text_lo()
    r_ip.wait()
    image_unit, image_inv = unit(ipart[0] + ipart[1])
    image_sent = image_unit.astype(BF16)
    place(all_image, image_sent)
    image_start()
    text_finish()

    image_grad = weigh(coefficients(image_sent, all_text), all_text)
    ig_out[...] = jnp.where(f == 0, image_grad[:rows], image_grad[rows:]).astype(BF16)
    image_back = back(image_unit, image_inv, image_grad).astype(BF16)
    d_pooled = mm_nt(image_back, hw0[...])
    grad_value = jnp.sum(d_pooled * pooled_raw, axis=0, keepdims=True)

    d_local = swap(d_pooled * sv_h)
    d_spread = (d_local[:, None, :] * head_mask[None]).reshape(n_ctx, half_d)
    direction = join(mm_nt(split(d_spread), vw[...]))
    m = group * heads
    blocks = []
    for side in range(2):
        for part in range(2):
            at = (side * 2 + part) * m
            d_att = join(mm_nt(split(direction[at : at + m]), tok[side, part * chunk : (part + 1) * chunk, :]))
            blocks.append(jnp.sum(d_att.reshape(group, heads, chunk) * block_mask, axis=0))
    d_att = jnp.concatenate(blocks, axis=1)
    a = jnp.concatenate([att[0], att[1]], axis=1)
    d_scores = split(a * (d_att - per_image(a * d_att, jnp.sum, 0.0)))
    mixed_keys = mm(d_scores[:, :half_tok], tok[0]) + mm(d_scores[:, half_tok:], tok[1])
    image_hi()
    image_lo()
    grad_key = join(mm(split(join(mixed_keys)), kw[...]))
    grad_key = probe_h * jnp.sum(grad_key * head_mask, axis=0, keepdims=True)

    tiles = half_d // 128

    def put(buf, x):
        buf[me] = jnp.zeros(buf.shape[1:], F32)
        n = x.shape[0]
        for j in range(tiles):
            buf[me, n * j : n * j + n, :] = x[:, 128 * j : 128 * j + 128]

    def total_copy(buf, slot, send, recv, k):
        return pltpu.make_async_remote_copy(
            src_ref=buf.at[slot], dst_ref=buf.at[slot], send_sem=send, recv_sem=recv,
            device_id=device(k), device_id_type=MESH,
        )

    def total_start(buf, send, recv):
        each(1, n_dev, lambda k: total_copy(buf, me, send.at[k], recv.at[me], k).start())

    def total_wait(buf, send, recv):
        def body(k):
            peer = lax.rem(me + k, n_dev)
            c = total_copy(buf, peer, send.at[k], recv.at[peer], k)
            c.wait_recv()
            c.wait_send()

        each(1, n_dev, body)

    put(fin_kv, jnp.concatenate([grad_key, grad_value], axis=0))
    total_start(fin_kv, kv_send, kv_recv)

    image_finish()
    text_grad = weigh(coefficients(text_sent, all_image), all_image)
    tg_out[...] = jnp.where(f == 0, text_grad[:rows], text_grad[rows:]).astype(BF16)
    grad_text = my_half(jnp.sum(back(text_unit, text_inv, text_grad) * text_raw, axis=0, keepdims=True))

    put(fin_text, grad_text)
    total_start(fin_text, ft_send, ft_recv)

    def write(buf, n, at):
        for side in range(2):
            total = buf[side]
            for k in range(1, n_dp):
                total = total + buf[2 * k + side]
            total = total * (1.0 / count)
            for j in range(tiles):
                start = side * half_d + 128 * j
                ia_out[at : at + n, start : start + 128] = total[n * j : n * j + n]

    total_wait(fin_kv, kv_send, kv_recv)
    write(fin_kv, 2, 0)
    total_wait(fin_text, ft_send, ft_recv)
    write(fin_text, 1, 2)


def hand_over(ig, tg, ia, ig_out, tg_out, ia_out):
    ig_out[...] = ig[...]
    tg_out[...] = tg[...]
    ia_out[...] = ia[...]


def on_device(n_dp, image_tokens, text_features, kv_weight, head_weight, probe, scale_key, scale_value, scale_text):
    rows, patches, d_model = image_tokens.shape
    half_d = kv_weight.shape[2]
    heads = half_d // HEAD_SIZE
    half_tok = rows * patches
    pair = 2 * rows
    count = n_dp * pair
    kv_rows, text_rows = (-(-n * half_d // 1024) * 8 for n in (2, 1))
    n_lo = 1
    n_hi = n_dp // n_lo
    dma = pltpu.SemaphoreType.DMA
    vec = (d_model,)
    vmem = pl.BlockSpec(memory_space=pltpu.VMEM)
    out_shape = (
        jax.ShapeDtypeStruct((rows, d_model), BF16),
        jax.ShapeDtypeStruct((rows, d_model), BF16),
        jax.ShapeDtypeStruct((3, d_model), F32),
    )
    results = pl.pallas_call(
        functools.partial(kernel, n_dp // n_lo, n_lo, rows),
        out_shape=out_shape,
        in_specs=[pl.BlockSpec(memory_space=pl.ANY)] * 8,
        out_specs=(vmem, vmem, vmem),
        scratch_shapes=[
            pltpu.VMEM((2, half_tok, d_model), BF16),
            pltpu.VMEM((d_model, half_d), BF16),
            pltpu.VMEM((d_model, half_d), BF16),
            pltpu.VMEM((half_d, d_model), BF16),
            pltpu.VMEM((half_d, d_model), BF16),
            pltpu.VMEM((rows, d_model), BF16),
            pltpu.VMEM((pair, d_model), F32),
            pltpu.VMEM(vec, F32),
            pltpu.VMEM(vec, F32),
            pltpu.VMEM(vec, F32),
            pltpu.VMEM(vec, F32),
            pltpu.VMEM((2, pair, d_model), F32),
            pltpu.VMEM((2, pair, d_model), F32),
            pltpu.VMEM((2, count, half_d), BF16),
            pltpu.VMEM((2, count, half_d), BF16),
            pltpu.VMEM((2, heads, half_tok), F32),
            pltpu.VMEM((2, pair * heads, d_model), BF16),
            pltpu.VMEM((2 * n_dp, kv_rows, 128), F32),
            pltpu.VMEM((2 * n_dp, text_rows, 128), F32),
            dma((11,)),
            dma((2,)),
            dma((2,)),
            dma((3,)),
            dma((3,)),
            [dma((n_hi,)), dma((n_dp,)), dma((n_dp,)), dma((n_dp,)), dma((n_dp,))],
            [dma((n_hi,)), dma((n_dp,)), dma((n_dp,)), dma((n_dp,)), dma((n_dp,))],
            dma((2 * n_dp,)),
            dma((2 * n_dp,)),
            dma((2 * n_dp,)),
            dma((2 * n_dp,)),
        ],
        compiler_params=pltpu.CompilerParams(
            collective_id=0, has_side_effects=True, vmem_limit_bytes=56 * 1024 * 1024
        ),
    )(
        image_tokens.reshape(half_tok, d_model), text_features, kv_weight, head_weight,
        probe, scale_key, scale_value, scale_text,
    )
    return pl.pallas_call(
        hand_over,
        out_shape=out_shape,
        in_specs=[vmem] * 3,
        out_specs=(vmem, vmem, vmem),
        compiler_params=pltpu.CompilerParams(vmem_limit_bytes=56 * 1024 * 1024),
    )(*results)


def solution(mesh):
    in_specs = (
        P(("group", "dp", "fsdp"), None, None),
        P(("group", "dp", "fsdp"), None),
        P(None, None, "fsdp"),
        P(None, "fsdp", None),
        P(),
        P(),
        P(),
        P(),
    )
    out_specs = (
        P(("group", "dp", "fsdp"), None),
        P(("group", "dp", "fsdp"), None),
        P("group", None),
    )
    return jax.shard_map(
        functools.partial(on_device, mesh.shape["dp"]),
        mesh=mesh, in_specs=in_specs, out_specs=out_specs, check_vma=False,
    )
```

```python
import functools
import math

import jax
import jax.numpy as jnp
from jax import lax
from jax.experimental import pallas as pl
from jax.experimental.pallas import tpu as pltpu
from jax.sharding import PartitionSpec as P

HEAD_SIZE = 96
PATCHES = 64
LOGIT_SCALE = 10.0
LOGIT_BIAS = -2.0
EPSILON = 1e-06
MESH = pl.DeviceIdType.MESH
BF16 = jnp.bfloat16
F32 = jnp.float32


def row(ref):
    return ref[...].reshape(1, ref.shape[0])


def mm(a, b):
    return jnp.dot(a, b, preferred_element_type=F32)


def mm_nt(a, b):
    return lax.dot_general(a, b, (((1,), (1,)), ((), ())), preferred_element_type=F32)


def split(x):
    high = x.astype(BF16)
    low = (x - high.astype(F32)).astype(BF16)
    return jnp.concatenate([high, low], axis=0)


def join(x):
    m = x.shape[0] // 2
    return x[:m] + x[m:]


def per_image(x, op, fill):
    lanes = lax.broadcasted_iota(jnp.int32, (x.shape[0], 128), 1)
    low = lanes < PATCHES
    blocks = []
    for j in range(x.shape[1] // 128):
        b = x[:, 128 * j : 128 * j + 128]
        first = op(jnp.where(low, b, fill), axis=1, keepdims=True)
        second = op(jnp.where(low, fill, b), axis=1, keepdims=True)
        blocks.append(jnp.where(low, first, second))
    return jnp.concatenate(blocks, axis=1)


def sigmoid(x):
    return 1.0 / (1.0 + jnp.exp(-x))


def kernel(
    n_hi, n_lo, rows, tok_hbm, txt_hbm, kv_hbm, hw_hbm, probe_hbm, sk_hbm, sv_hbm, st_hbm,
    ig_out, tg_out, ia_out,
    tok, kw, vw, hw0, hw1, txt_in, txt, probe, sk, sv, st, tpart, ipart, all_text, all_image,
    att, ctx, fin_kv, fin_text, last, local_sem, tok_send, tok_recv, pair_send, pair_recv,
    text_sems, image_sems, kv_send, kv_recv, ft_send, ft_recv,
):
    dp = lax.axis_index("dp")
    f = lax.axis_index("fsdp")
    other = 1 - f
    hi, lo = dp // n_lo, lax.rem(dp, n_lo)
    n_dp = n_hi * n_lo
    d_model = tok.shape[2]
    half_d = kw.shape[1]
    heads = half_d // HEAD_SIZE
    pair = 2 * rows
    half_tok = rows * PATCHES
    chunk = half_tok // 2
    count = n_dp * pair

    copies = []

    def load(src, dst):
        c = pltpu.make_async_copy(src, dst, local_sem.at[len(copies)])
        c.start()
        copies.append(c)
        return c

    c_txt = load(txt_hbm, txt_in)
    c_vec = [load(probe_hbm, probe), load(sk_hbm, sk), load(sv_hbm, sv), load(st_hbm, st)]
    c_kw = load(kv_hbm.at[0], kw)
    c_hw1 = load(hw_hbm.at[1], hw1)
    c_tok = [
        load(tok_hbm.at[pl.ds(chunk * i, chunk)], tok.at[0, pl.ds(chunk * i, chunk)]) for i in range(2)
    ]
    c_vw = load(kv_hbm.at[1], vw)
    c_hw0 = load(hw_hbm.at[0], hw0)

    barrier = pltpu.get_barrier_semaphore()


    def each(low, high, body):
        def step(k, carry):
            body(k)
            return carry

        lax.fori_loop(low, high, step, 0)

    def device(k):
        return {"dp": lax.rem(dp + k, n_dp), "fsdp": f}

    pl.semaphore_signal(barrier, inc=1, device_id={"fsdp": other}, device_id_type=MESH)
    each(
        1, n_dp,
        lambda k: pl.semaphore_signal(barrier, inc=1, device_id=device(k), device_id_type=MESH),
    )

    c_txt.wait()
    mine = pl.ds(pl.multiple_of(f * rows, rows), rows)
    txt[mine, :] = txt_in[...].astype(F32)

    def my_half(v):
        return jnp.where(f == 0, v[:, :half_d], v[:, half_d:])

    row_id = lax.broadcasted_iota(jnp.int32, (heads, half_d), 0)
    col_id = lax.broadcasted_iota(jnp.int32, (heads, half_d), 1)
    head_mask = ((col_id >= row_id * HEAD_SIZE) & (col_id < (row_id + 1) * HEAD_SIZE)).astype(F32)

    for c in c_vec:
        c.wait()
    probe_h = my_half(row(probe)) * (1.0 / math.sqrt(HEAD_SIZE))
    sv_h = my_half(row(sv))
    query = head_mask * (probe_h * my_half(row(sk)))
    c_kw.wait()
    query_tok = split(join(mm_nt(split(query), kw[...])))

    pl.semaphore_wait(barrier, n_dp)

    def to_partner(src, dst, send, recv):
        return pltpu.make_async_remote_copy(
            src_ref=src, dst_ref=dst, send_sem=send, recv_sem=recv,
            device_id={"fsdp": other}, device_id_type=MESH,
        )

    r_txt = to_partner(txt.at[mine], txt.at[mine], pair_send.at[0], pair_recv.at[0])
    r_txt.start()
    r_tok = []
    for i in range(2):
        r = to_partner(
            tok_hbm.at[pl.ds(chunk * i, chunk)], tok.at[1, pl.ds(chunk * i, chunk)],
            tok_send.at[i], tok_recv.at[i],
        )
        r.start()
        r_tok.append(r)

    def unit(e):
        inv = lax.rsqrt(jnp.sum(e * e, axis=1, keepdims=True) + EPSILON)
        return e * inv, inv

    def back(u, inv, g):
        return inv * (g - u * jnp.sum(u * g, axis=1, keepdims=True))

    my_rows = pl.ds(pl.multiple_of(dp * pair, pair), pair)

    def gather_copy(buf, side, origin, send, recv, peer, core):
        block = buf.at[side, pl.ds(pl.multiple_of(origin * pair, pair), pair)]
        return pltpu.make_async_remote_copy(
            src_ref=block, dst_ref=block, send_sem=send, recv_sem=recv,
            device_id={"dp": peer, "fsdp": core}, device_id_type=MESH,
        )

    def gather(buf, sems):
        hi_send, lo_send, recv, core_send, core_recv = sems

        def to_hi(k):
            h = lax.rem(hi + k, n_hi)
            return gather_copy(buf, f, dp, hi_send.at[h], recv.at[dp], h * n_lo + lo, f)

        def to_lo(h, k):
            t = lax.rem(lo + k, n_lo)
            origin = h * n_lo + lo
            return gather_copy(buf, f, origin, lo_send.at[h * n_lo + t], recv.at[origin], hi * n_lo + t, f)

        def to_core(origin):
            return gather_copy(buf, f, origin, core_send.at[origin], core_recv.at[origin], dp, other)

        def arrived(origin):
            gather_copy(buf, f, origin, hi_send.at[0], recv.at[origin], dp, other).wait_recv()

        def start():
            each(1, n_hi, lambda k: to_hi(k).start())
            each(1, n_lo, lambda k: to_lo(hi, k).start())

        def forward_hi():
            def body(k):
                h = lax.rem(hi + k, n_hi)
                arrived(h * n_lo + lo)
                each(1, n_lo, lambda j: to_lo(h, j).start())
                to_core(h * n_lo + lo).start()

            each(1, n_hi, body)

        def forward_lo():
            def body(k):
                def inner(j):
                    origin = lax.rem(hi + j, n_hi) * n_lo + lax.rem(lo + k, n_lo)
                    arrived(origin)
                    to_core(origin).start()

                each(0, n_hi, inner)

            each(1, n_lo, body)

        def finish():
            def cores(k):
                origin = lax.rem(dp + k, n_dp)
                gather_copy(buf, other, origin, core_send.at[origin], core_recv.at[origin], dp, other).wait_recv()

            def sent(k):
                to_core(lax.rem(dp + k, n_dp)).wait_send()

            each(1, n_dp, cores)
            each(1, n_dp, sent)
            each(1, n_hi, lambda k: to_hi(k).wait_send())
            each(0, n_hi, lambda h: each(1, n_lo, lambda k: to_lo(h, k).wait_send()))

        return start, forward_hi, forward_lo, finish

    def place(buf, sent):
        buf[0, my_rows, :] = sent[:, :half_d]
        buf[1, my_rows, :] = sent[:, half_d:]

    def similarity(sent, buf):
        return mm_nt(sent[:, :half_d], buf[0]) + mm_nt(sent[:, half_d:], buf[1])

    def weigh(coeffs, buf):
        return LOGIT_SCALE * jnp.concatenate([mm(coeffs, buf[0]), mm(coeffs, buf[1])], axis=1)

    text_start, text_hi, text_lo, text_finish = gather(all_text, text_sems)
    image_start, image_hi, image_lo, image_finish = gather(all_image, image_sems)

    c_hw1.wait()
    r_txt.wait()
    t_all = txt[...]
    tpart[0] = mm(my_half(t_all).astype(BF16), hw1[...])
    r_tp = to_partner(tpart.at[0], tpart.at[1], pair_send.at[1], pair_recv.at[1])
    r_tp.start()

    group = chunk // PATCHES
    ga = lax.broadcasted_iota(jnp.int32, (group, heads, chunk), 0) * PATCHES
    gb = lax.broadcasted_iota(jnp.int32, (group, heads, chunk), 2)
    block_mask = ((gb >= ga) & (gb < ga + PATCHES)).astype(F32)

    def attend(side):
        scores = join(mm_nt(query_tok, tok[side]))
        e = jnp.exp(scores - per_image(scores, jnp.max, -jnp.inf))
        a = e / per_image(e, jnp.sum, 0.0)
        att[side] = a
        m = group * heads
        for part in range(2):
            spread = (a[None, :, part * chunk : (part + 1) * chunk] * block_mask).reshape(m, chunk)
            mixed = split(join(mm(split(spread), tok[side, part * chunk : (part + 1) * chunk, :])))
            at = (side * 2 + part) * m
            ctx[0, at : at + m, :] = mixed[:m]
            ctx[1, at : at + m, :] = mixed[m:]

    c_tok[0].wait()
    c_tok[1].wait()
    attend(0)

    r_tp.wait()
    text_raw = tpart[0] + tpart[1]
    text_unit, text_inv = unit(text_raw * row(st))
    text_sent = text_unit.astype(BF16)
    place(all_text, text_sent)
    text_start()

    r_tok[0].wait()
    r_tok[1].wait()
    attend(1)

    def swap(x):
        m = x.shape[0] // 2
        return jnp.where(f == 0, x, jnp.concatenate([x[m:], x[:m]], axis=0))

    c_vw.wait()
    n_ctx = pair * heads
    pooled_all = mm(ctx[...].reshape(2 * n_ctx, d_model), vw[...])
    pooled_all = join(pooled_all).reshape(pair, heads, half_d) * head_mask[None]
    pooled_raw = swap(jnp.sum(pooled_all, axis=1))
    pooled = (pooled_raw * sv_h).astype(BF16)
    c_hw0.wait()
    ipart[0] = mm(pooled, hw0[...])
    r_ip = to_partner(ipart.at[0], ipart.at[1], pair_send.at[2], pair_recv.at[2])
    r_ip.start()

    d_row = lax.broadcasted_iota(jnp.int32, (pair, count), 0) + dp * pair
    d_col = lax.broadcasted_iota(jnp.int32, (pair, count), 1)
    diagonal = (d_row == d_col).astype(F32)

    def coefficients(sent, buf):
        logits = LOGIT_SCALE * similarity(sent, buf) + LOGIT_BIAS
        return (sigmoid(logits) - diagonal).astype(BF16)

    text_hi()
    text_lo()
    r_ip.wait()
    image_unit, image_inv = unit(ipart[0] + ipart[1])
    image_sent = image_unit.astype(BF16)
    place(all_image, image_sent)
    image_start()
    text_finish()

    image_grad = weigh(coefficients(image_sent, all_text), all_text)
    ig_out[...] = jnp.where(f == 0, image_grad[:rows], image_grad[rows:]).astype(BF16)
    image_back = back(image_unit, image_inv, image_grad).astype(BF16)
    d_pooled = mm_nt(image_back, hw0[...])
    grad_value = jnp.sum(d_pooled * pooled_raw, axis=0, keepdims=True)

    d_local = swap(d_pooled * sv_h)
    d_spread = (d_local[:, None, :] * head_mask[None]).reshape(n_ctx, half_d)
    direction = join(mm_nt(split(d_spread), vw[...]))
    m = group * heads
    blocks = []
    for side in range(2):
        for part in range(2):
            at = (side * 2 + part) * m
            d_att = join(mm_nt(split(direction[at : at + m]), tok[side, part * chunk : (part + 1) * chunk, :]))
            blocks.append(jnp.sum(d_att.reshape(group, heads, chunk) * block_mask, axis=0))
    d_att = jnp.concatenate(blocks, axis=1)
    a = jnp.concatenate([att[0], att[1]], axis=1)
    d_scores = split(a * (d_att - per_image(a * d_att, jnp.sum, 0.0)))
    mixed_keys = mm(d_scores[:, :half_tok], tok[0]) + mm(d_scores[:, half_tok:], tok[1])
    image_hi()
    image_lo()
    grad_key = join(mm(split(join(mixed_keys)), kw[...]))
    grad_key = probe_h * jnp.sum(grad_key * head_mask, axis=0, keepdims=True)

    tiles = half_d // 128

    def put(buf, x):
        buf[dp] = jnp.zeros(buf.shape[1:], F32)
        n = x.shape[0]
        for j in range(tiles):
            buf[dp, n * j : n * j + n, :] = x[:, 128 * j : 128 * j + 128]

    def total_copy(buf, slot, send, recv, k):
        return pltpu.make_async_remote_copy(
            src_ref=buf.at[slot], dst_ref=buf.at[slot], send_sem=send, recv_sem=recv,
            device_id=device(k), device_id_type=MESH,
        )

    def total_start(buf, send, recv):
        each(1, n_dp, lambda k: total_copy(buf, dp, send.at[k], recv.at[dp], k).start())

    def total_wait(buf, send, recv):
        def body(k):
            peer = lax.rem(dp + k, n_dp)
            c = total_copy(buf, peer, send.at[k], recv.at[peer], k)
            c.wait_recv()
            c.wait_send()

        each(1, n_dp, body)

    put(fin_kv, jnp.concatenate([grad_key, grad_value], axis=0))
    total_start(fin_kv, kv_send, kv_recv)

    image_finish()
    text_grad = weigh(coefficients(text_sent, all_image), all_image)
    tg_out[...] = jnp.where(f == 0, text_grad[:rows], text_grad[rows:]).astype(BF16)
    grad_text = my_half(jnp.sum(back(text_unit, text_inv, text_grad) * text_raw, axis=0, keepdims=True))

    put(fin_text, grad_text)
    total_start(fin_text, ft_send, ft_recv)

    total_wait(fin_kv, kv_send, kv_recv)
    kv_rows = fin_kv.shape[1]
    last[f, :kv_rows, :] = jnp.sum(fin_kv[...], axis=0)
    total_wait(fin_text, ft_send, ft_recv)
    last[f, kv_rows:, :] = jnp.sum(fin_text[...], axis=0)
    to_partner(last.at[f], last.at[f], pair_send.at[3], pair_recv.at[3]).start()
    to_partner(last.at[other], last.at[other], pair_send.at[3], pair_recv.at[3]).wait()
    for side in range(2):
        total = last[side] * (1.0 / count)
        for j in range(tiles):
            start = side * half_d + 128 * j
            ia_out[0:2, start : start + 128] = total[2 * j : 2 * j + 2]
            ia_out[2:3, start : start + 128] = total[kv_rows + j : kv_rows + j + 1]


def hand_over(ig, tg, ia, ig_out, tg_out, ia_out):
    ig_out[...] = ig[...]
    tg_out[...] = tg[...]
    ia_out[...] = ia[...]


def on_device(n_dp, image_tokens, text_features, kv_weight, head_weight, probe, scale_key, scale_value, scale_text):
    rows, patches, d_model = image_tokens.shape
    half_d = kv_weight.shape[2]
    heads = half_d // HEAD_SIZE
    half_tok = rows * patches
    pair = 2 * rows
    count = n_dp * pair
    kv_rows, text_rows = (-(-n * half_d // 1024) * 8 for n in (2, 1))
    n_lo = 1
    n_hi = n_dp // n_lo
    dma = pltpu.SemaphoreType.DMA
    vec = (d_model,)
    vmem = pl.BlockSpec(memory_space=pltpu.VMEM)
    out_shape = (
        jax.ShapeDtypeStruct((rows, d_model), BF16),
        jax.ShapeDtypeStruct((rows, d_model), BF16),
        jax.ShapeDtypeStruct((3, d_model), F32),
    )
    results = pl.pallas_call(
        functools.partial(kernel, n_dp // n_lo, n_lo, rows),
        out_shape=out_shape,
        in_specs=[pl.BlockSpec(memory_space=pl.ANY)] * 8,
        out_specs=(vmem, vmem, vmem),
        scratch_shapes=[
            pltpu.VMEM((2, half_tok, d_model), BF16),
            pltpu.VMEM((d_model, half_d), BF16),
            pltpu.VMEM((d_model, half_d), BF16),
            pltpu.VMEM((half_d, d_model), BF16),
            pltpu.VMEM((half_d, d_model), BF16),
            pltpu.VMEM((rows, d_model), BF16),
            pltpu.VMEM((pair, d_model), F32),
            pltpu.VMEM(vec, F32),
            pltpu.VMEM(vec, F32),
            pltpu.VMEM(vec, F32),
            pltpu.VMEM(vec, F32),
            pltpu.VMEM((2, pair, d_model), F32),
            pltpu.VMEM((2, pair, d_model), F32),
            pltpu.VMEM((2, count, half_d), BF16),
            pltpu.VMEM((2, count, half_d), BF16),
            pltpu.VMEM((2, heads, half_tok), F32),
            pltpu.VMEM((2, pair * heads, d_model), BF16),
            pltpu.VMEM((n_dp, kv_rows, 128), F32),
            pltpu.VMEM((n_dp, text_rows, 128), F32),
            pltpu.VMEM((2, kv_rows + text_rows, 128), F32),
            dma((11,)),
            dma((2,)),
            dma((2,)),
            dma((4,)),
            dma((4,)),
            [dma((n_hi,)), dma((n_dp,)), dma((n_dp,)), dma((n_dp,)), dma((n_dp,))],
            [dma((n_hi,)), dma((n_dp,)), dma((n_dp,)), dma((n_dp,)), dma((n_dp,))],
            dma((n_dp,)),
            dma((n_dp,)),
            dma((n_dp,)),
            dma((n_dp,)),
        ],
        compiler_params=pltpu.CompilerParams(
            collective_id=0, has_side_effects=True, vmem_limit_bytes=56 * 1024 * 1024
        ),
    )(
        image_tokens.reshape(half_tok, d_model), text_features, kv_weight, head_weight,
        probe, scale_key, scale_value, scale_text,
    )
    return pl.pallas_call(
        hand_over,
        out_shape=out_shape,
        in_specs=[vmem] * 3,
        out_specs=(vmem, vmem, vmem),
        compiler_params=pltpu.CompilerParams(vmem_limit_bytes=56 * 1024 * 1024),
    )(*results)


def solution(mesh):
    in_specs = (
        P(("group", "dp", "fsdp"), None, None),
        P(("group", "dp", "fsdp"), None),
        P(None, None, "fsdp"),
        P(None, "fsdp", None),
        P(),
        P(),
        P(),
        P(),
    )
    out_specs = (
        P(("group", "dp", "fsdp"), None),
        P(("group", "dp", "fsdp"), None),
        P("group", None),
    )
    return jax.shard_map(
        functools.partial(on_device, mesh.shape["dp"]),
        mesh=mesh, in_specs=in_specs, out_specs=out_specs, check_vma=False,
    )
```
